768 devices in a mesh: dp: 32 (over y, x), mp: 24 (over z, core).
Axes of the slice: x: 4, y: 8, z: 12, core: 2. Of those that a mesh axis runs over, the one named last changes fastest.
Arguments:
- patches: bfloat16 [9216, 6144], P('dp', 'mp'), may hold values from -6 to 6
- pack_route: int32 [9216, 1], P('dp'), may hold values from 0 to 31, as said below
- pack_slot: int32 [9216, 1], P('dp'), may hold values from 0 to 383, as said below
- project_weight: bfloat16 [6144, 9216], P(None, 'mp'), may hold values from -0.078125 to 0.078125
- cotangent: bfloat16 [12288, 3072], P('dp', 'mp'), may hold values from -6 to 6
Outputs:
- attention: bfloat16 [12288, 3072], P('dp', 'mp')
- weight_grad: float32 [6144, 9216], P('dp', 'mp')
The draws below stay inside these ranges and needn't reach their ends.
Inputs may be any that keep to these rules, and one draw needn't show every extreme that they name: `pack_route`: loader shard s holds rows s * 288 to (s + 1) * 288 - 1. Each shard sends 288 rows in all and each pack receives 288 rows; among the rows of one shard at most 18 name the same pack, and every shard names some pack exactly 18 times. `pack_slot`: rows that name the same pack name different slots; within each block of 96 slots of a pack the named slots are the first ones; some image fills all 96 slots of its block, in the first block of some pack and in the second block of another.
All inputs are finite; a program needn't handle non-finite values.
Results may differ from the reference program's by a relative error of at most 0.024.
Values may be sent and summed in bfloat16 or wider, within the bound.
No kernel may reach another device: no remote copies, remote signals or barrier semaphores. Data moves between devices by JAX's collectives and lax.ppermute only.
A program may use at most 32 MiB of HBM per device.

```python
import jax
import jax.numpy as jnp
from jax import lax

D = 6144
HD = 128
CAP = 96
IMGS = 4
HEADS = 24
ROWS_DEV = 288
SLOTS = 384
ROWS = 9216
N_DP = 32


def pack_layout(key):
    owners = N_DP
    share = ROWS_DEV // owners
    total = owners * ROWS_DEV
    half = owners // 2
    half_rows = 3 * CAP // 2
    pair_count = IMGS // 2
    keys = jax.random.split(key, 10)
    diffs = jax.random.randint(keys[0], (half,), -share, share + 1, dtype=jnp.int32)
    chosen = jax.random.randint(keys[1], (), 0, half, dtype=jnp.int32)
    diffs = jnp.where(jnp.arange(half, dtype=jnp.int32) == chosen, share, diffs)
    paired = jnp.stack([share + diffs, share - diffs], axis=1).reshape(owners)
    spread = paired[jax.random.permutation(keys[2], owners)]
    row_perm = jax.random.permutation(keys[3], owners).astype(jnp.int32)
    col_perm = jax.random.permutation(keys[4], owners).astype(jnp.int32)
    sends = spread[(row_perm[:, None] + col_perm[None, :]) % owners]
    indices = jnp.arange(owners, dtype=jnp.int32)
    first_len = jax.random.randint(keys[5], (owners, pair_count), half_rows - CAP, CAP + 1, dtype=jnp.int32)
    full_one = jax.random.randint(keys[6], (), 0, owners, dtype=jnp.int32)
    full_two = (full_one + 1 + jax.random.randint(keys[7], (), 0, owners - 1, dtype=jnp.int32)) % owners
    column_zero = jnp.where(indices == full_one, CAP, jnp.where(indices == full_two, half_rows - CAP, first_len[:, 0]))
    first_len = first_len.at[:, 0].set(column_zero)
    places = jnp.arange(ROWS_DEV, dtype=jnp.int32)
    pair_of = places // half_rows
    local_place = places % half_rows
    first_here = first_len[:, pair_of]
    bounds = jnp.cumsum(sends, axis=1)
    source = jnp.sum((bounds[:, None, :] <= places[None, :, None]).astype(jnp.int32), axis=2)
    second = (local_place[None, :] >= first_here).astype(jnp.int32)
    slot = pair_of[None, :] * (2 * CAP) + second * CAP + local_place[None, :] - second * first_here
    shuffles = jax.vmap(lambda k: jax.random.permutation(k, ROWS_DEV))(jax.random.split(keys[8], owners))
    slot = jnp.take_along_axis(slot, shuffles.astype(jnp.int32), axis=1)
    owner_of = jnp.broadcast_to(indices[:, None], (owners, ROWS_DEV))
    ranks = jax.random.permutation(keys[9], total).astype(jnp.int32)
    sort_key = source.reshape(-1) * total + ranks
    order = jnp.argsort(sort_key)
    routes = owner_of.reshape(-1)[order].reshape(total, 1).astype(jnp.int32)
    slots = slot.reshape(-1)[order].reshape(total, 1).astype(jnp.int32)
    return (routes, slots)


def draw_pack_route(key, part):
    return pack_layout(key)[0]


def draw_pack_slot(key, part):
    return pack_layout(key)[1]


def block_levels(rng, dims, cuts, least, largest):
    gain, own = 1.0, jax.random.fold_in(rng, 6)
    for dim, parts in cuts:
        steps = jnp.exp(jax.random.uniform(jax.random.fold_in(own, dim), (parts,), jnp.float32, least / len(cuts), largest / len(cuts)))
        gain = gain * jnp.repeat(steps, dims[dim] // parts).reshape([-1 if axis == dim else 1 for axis in range(len(dims))])
    return gain


def scatter_about(rng, dims, scale, most, cuts=(), held_as=jnp.bfloat16):
    values = scale * jax.random.normal(rng, dims, jnp.float32)
    if cuts:
        values = values * block_levels(rng, dims, cuts, -0.22, 0.18)
    return jnp.clip(values, -most, most).astype(held_as)


def setup_inputs(seed: int = 0) -> dict:
    seeds = jax.random.split(jax.random.key(seed), 6)
    return {
        "patches": scatter_about(seeds[0], (ROWS, D), 1.0, 6.0, ((0, 32), (1, 24))),
        "pack_route": draw_pack_route(jax.random.fold_in(seeds[5], 71), 0),
        "pack_slot": draw_pack_slot(jax.random.fold_in(seeds[5], 71), 0),
        "project_weight": scatter_about(seeds[3], (D, 3 * HD * HEADS), D ** -0.5, 0.078125, ((1, 24),)),
        "cotangent": scatter_about(seeds[4], (N_DP * SLOTS, HD * HEADS), 1.0, 6.0, ((0, 32), (1, 24))),
    }


def attend(projected, filled):
    blocks = filled.shape[0]
    capacity = projected.shape[0] // blocks
    head_width_dim = projected.shape[1] // 3
    rounded = projected.astype(jnp.bfloat16).reshape(blocks, capacity, 3, head_width_dim)
    query_matrix = rounded[:, :, 0].astype(jnp.float32)
    key_matrix = rounded[:, :, 1].astype(jnp.float32)
    value_matrix = rounded[:, :, 2].astype(jnp.float32)
    logit_scores = jnp.einsum('lnw,lcw->lnc', query_matrix, key_matrix) * head_width_dim ** (-0.5)
    valid_token_mask = (jnp.arange(capacity, dtype=jnp.int32)[None, :] < filled[:, None]).astype(jnp.float32)
    expscore = jnp.exp(logit_scores) * valid_token_mask[:, None, :]
    denominator = lax.optimization_barrier(jnp.sum(expscore, axis=-1)) + (1.0 - valid_token_mask)
    softmax_weights = (expscore / denominator[..., None]).astype(jnp.bfloat16)
    attended_values = jnp.einsum('fnp,fpg->fng', softmax_weights.astype(jnp.float32), value_matrix) * valid_token_mask[..., None]
    return attended_values.astype(jnp.bfloat16).reshape(blocks * capacity, head_width_dim)

def reference(patches, pack_route, pack_slot, project_weight, cotangent):
    owners = N_DP
    slot_count = SLOTS
    routes = pack_route[:, 0].astype(jnp.int32)
    slots = pack_slot[:, 0].astype(jnp.int32)
    target = routes * slot_count + slots
    packed = jnp.zeros((owners * slot_count, D), jnp.bfloat16).at[target].set(patches)
    image_id = routes * IMGS + slots // CAP
    image_ids = jnp.arange(owners * IMGS, dtype=jnp.int32)
    filled_all = lax.optimization_barrier(jnp.sum((image_id[:, None] == image_ids[None, :]).astype(jnp.int32), axis=0)).reshape(owners, IMGS)

    def one_owner(accum, inputs):
        rows_here, filled, grad_here = inputs
        projected = jnp.dot(rows_here, project_weight, preferred_element_type=jnp.float32)
        by_head = jnp.transpose(projected.reshape(slot_count, HEADS, 3 * HD), (1, 0, 2))
        grad_heads = jnp.transpose(grad_here.reshape(slot_count, HEADS, HD), (1, 0, 2))

        def per_head(values_in, grad_in):
            result, pull = jax.vjp(lambda z: attend(z, filled), values_in)
            return (result, pull(grad_in)[0].astype(jnp.bfloat16))
        results, grads = jax.vmap(per_head)(by_head, grad_heads)
        grad_flat = jnp.transpose(grads, (1, 0, 2)).reshape(slot_count, HEADS * 3 * HD)
        weight_term = jnp.dot(rows_here.T, grad_flat, preferred_element_type=jnp.float32)
        accum = accum + lax.optimization_barrier(weight_term.astype(jnp.bfloat16)).astype(jnp.float32)
        return (accum, jnp.transpose(results, (1, 0, 2)).reshape(slot_count, HEADS * HD))
    initial = jnp.zeros((D, 3 * HD * HEADS), jnp.float32)
    weight_grad, outputs = lax.scan(one_owner, initial, (packed.reshape(owners, slot_count, D), filled_all, cotangent.reshape(owners, slot_count, HD * HEADS)))
    return (outputs.reshape(owners * slot_count, HD * HEADS), weight_grad)
```

```python
import jax
import jax.numpy as jnp
from jax import lax
from jax.experimental import pallas as pl
from jax.experimental.pallas import tpu as pltpu
from jax.sharding import PartitionSpec as P

CAP = 96
HD = 128
SENT = 18
ROOM = 24
X, Y = 4, 8
F32, BF16, I32 = jnp.float32, jnp.bfloat16, jnp.int32


def iota(shape, dim):
    return lax.broadcasted_iota(I32, shape, dim)


def hot(condition):
    return jnp.where(condition, 1.0, 0.0).astype(BF16)


def mm(a, b, ca=1, cb=0):
    return lax.dot_general(a, b, (((ca,), (cb,)), ((), ())), preferred_element_type=F32)


def send_kernel(patches, route, slot, out):
    rows = patches.shape[0]
    owners = out.shape[0] // ROOM
    pack = route[...]
    place = slot[...]
    matches = hot(pack == iota((rows, owners), 1))
    before = mm(hot(iota((rows, rows), 0) > iota((rows, rows), 1)), matches)
    position = jnp.sum(before * matches.astype(F32), axis=1, keepdims=True).astype(I32)
    spread = hot(pack * ROOM + position == iota((rows, owners * ROOM), 1))
    total = mm(spread, patches[...], 0, 0)
    held = hot(position == iota((rows, 256), 1)).astype(F32)
    high = (held * ((place >> 1) + 1).astype(F32)).astype(BF16)
    low = (held * (place & 1).astype(F32)).astype(BF16)
    line, owner = iota((owners * ROOM, owners), 0), iota((owners * ROOM, owners), 1)
    for row, part in ((SENT, high), (SENT + 1, low)):
        total += mm(hot(line == owner * ROOM + row), mm(matches, part, 0, 0).astype(BF16))
    out[...] = total.astype(BF16)


def receive_kernel(arrived, out, offsets):
    lines = arrived.shape[0]
    owners = lines // ROOM
    rows = out.shape[0]
    data = arrived[...]
    line, owner = iota((owners, lines), 1), iota((owners, lines), 0)
    spread = hot((line >= owner * ROOM) & (line < owner * ROOM + ROOM))
    within = jnp.sum(
        jnp.where((line >= owner * ROOM) & (line < owner * ROOM + ROOM), line - owner * ROOM, 0),
        axis=0,
        keepdims=True,
    )
    chosen = iota((128, lines), 0) == within
    number = []
    for row in (SENT, SENT + 1):
        part = mm(hot(line == owner * ROOM + row), data)[:, :128].astype(BF16)
        wide = mm(part, spread, 0, 0)
        number.append(jnp.sum(jnp.where(chosen, wide, 0.0), axis=0, keepdims=True).astype(I32))
    live = (number[0] > 0) & (within < SENT)
    place = 2 * (number[0] - 1) + number[1]
    image = sum((place >= CAP * j).astype(I32) for j in (1, 2, 3))
    start, starts, base = jnp.zeros((1, 1), I32), [], jnp.zeros_like(place)
    for j in range(3):
        count = jnp.sum(jnp.where(live & (image == j), 1.0, 0.0), axis=1, keepdims=True)
        start = start + count.astype(I32)
        starts.append(start)
        base = jnp.where(image == j + 1, start, base)
    target = jnp.where(live, base + place - CAP * image, -1)
    out[...] = mm(hot(iota((rows, lines), 0) == target), data).astype(BF16)
    lane = iota((8, 128), 1)
    offsets[...] = sum(jnp.where(lane == j, starts[j], 0) for j in range(3))


def places(index, offsets):
    image, base, last = 0, 0, 0
    for j in range(3):
        start = offsets[0:1, j : j + 1]
        past = index >= start
        image = image + past.astype(I32)
        base = base + jnp.where(past, start - last, 0)
        last = start
    return image, index - base + CAP * image


def attend_kernel(features, weight, cotangent, offsets, attention, grads, total):
    step = pl.program_id(0)
    part = mm(features[0], weight[0])
    for k in range(1, features.shape[0]):
        part += mm(features[k], weight[k])

    @pl.when(step == 0)
    def _():
        total[...] = part

    @pl.when(step > 0)
    def _():
        total[...] += part

    @pl.when(step == pl.num_programs(0) - 1)
    def _():
        rows, slots = total.shape[0], attention.shape[0]
        offs = offsets[...]
        image_col, slot_col = places(iota((rows, 1), 0), offs)
        image_row, slot_row = places(iota((1, rows), 1), offs)
        same = image_col == image_row
        cot = mm(hot(slot_col == iota((rows, slots), 1)), cotangent[...]).astype(BF16)
        rounded = total[...].astype(BF16)
        query, key, value = rounded[:, :HD], rounded[:, HD : 2 * HD], rounded[:, 2 * HD :]
        scale = HD ** (-0.5)
        scores = mm(query, key, 1, 1) * scale
        expscore = jnp.where(same, jnp.exp(jnp.where(same, scores, 0.0)), 0.0)
        softmax = expscore / jnp.sum(expscore, axis=1, keepdims=True)
        weights = softmax.astype(BF16)
        result = mm(weights, value).astype(BF16)
        attention[...] = mm(hot(iota((slots, rows), 0) == slot_row), result).astype(BF16)
        d_value = mm(weights, cot, 0, 0)
        d_weights = mm(cot, value, 1, 1).astype(BF16).astype(F32)
        d_weights = jnp.where(same, d_weights, 0.0)
        inner = jnp.sum(d_weights * softmax, axis=1, keepdims=True)
        d_scores = (softmax * (d_weights - inner) * scale).astype(BF16)
        grads[:, :HD] = mm(d_scores, key).astype(BF16)
        grads[:, HD : 2 * HD] = mm(d_scores, query, 0, 0).astype(BF16)
        grads[:, 2 * HD :] = d_value.astype(BF16)


def split_kernel(core, features, out):
    def tile(t):
        return features[t // 2, :, (t % 2) * 128 : (t % 2) * 128 + 128]

    row, col = iota((256, 128), 0), iota((256, 128), 1)
    near = hot(row == jnp.where(col < 64, col, col + 64))
    far = hot(row == jnp.where(col < 64, col + 64, col + 128))
    for x, (whole, cut, pick) in enumerate(((0, 1, near), (2, 1, far), (3, 4, near), (5, 4, far))):
        out[x, :, 0:128] = tile(whole)
        out[x, :, 128:256] = tile(whole + 6)
        both = jnp.concatenate([tile(cut), tile(cut + 6)], axis=1)
        out[x, :, 256:384] = mm(both, pick).astype(BF16)


def weight_kernel(core, own, other, grads, out):
    depth = grads.shape[0] * grads.shape[1]
    right = grads[...].reshape(depth, grads.shape[2])
    for source, side in ((own, core[0]), (other, 1 - core[0])):
        for a in range(2):
            left = source[:, :, a * 384 : a * 384 + 384].reshape(depth, 384)
            term = mm(left, right, 0, 0).astype(BF16)
            at = side * 4 + a * 2
            for b in range(2):
                out[at + b, 0:128] = term[b * 128 : b * 128 + 128]
                out[at + b, 128:192] = term[256 + b * 64 : 320 + b * 64]


def sum_kernel(odd, terms, out):
    total = terms[0].astype(F32)
    for k in range(1, terms.shape[0]):
        total += terms[k].astype(F32)

    @pl.when(odd[0] == 0)
    def _():
        out[...] = total

    @pl.when(odd[0] == 1)
    def _():
        out[0:64] = total[128:192]
        out[64:192] = total[0:128]


def params():
    return pltpu.CompilerParams(vmem_limit_bytes=40 * 1024 * 1024)


def cost(flops, moved):
    return pl.CostEstimate(flops=flops, bytes_accessed=moved, transcendentals=0)


VMEM = pl.BlockSpec(memory_space=pltpu.VMEM)
SMEM = pl.BlockSpec(memory_space=pltpu.SMEM)


def shards(patches, pack_route, pack_slot, project_weight, cotangent):
    owners, heads = lax.axis_size("dp"), lax.axis_size("mp")
    rows, width = patches.shape
    slots = cotangent.shape[0]
    cols = project_weight.shape[1]
    core = (lax.axis_index("mp") % 2).astype(I32).reshape(1)
    odd = (lax.axis_index("dp") % 2).astype(I32).reshape(1)
    along_x = [[y * X + x for x in range(X)] for y in range(Y)]
    along_y = [[y * X + x for y in range(Y)] for x in range(X)]

    outgoing = pl.pallas_call(
        send_kernel,
        out_shape=jax.ShapeDtypeStruct((owners * ROOM, width), BF16),
        in_specs=[VMEM] * 3,
        out_specs=VMEM,
        compiler_params=params(),
        name="send",
    )(patches, pack_route, pack_slot)
    arrived = lax.all_to_all(outgoing.reshape(owners, ROOM, width), "dp", 0, 0, tiled=True)
    compact, offsets = pl.pallas_call(
        receive_kernel,
        out_shape=(
            jax.ShapeDtypeStruct((rows, width), BF16),
            jax.ShapeDtypeStruct((8, 128), I32),
        ),
        in_specs=[VMEM],
        out_specs=(VMEM, VMEM),
        compiler_params=params(),
        name="receive",
    )(arrived.reshape(owners * ROOM, width))

    features = lax.all_gather(compact, "mp", axis=0)

    part = heads // 4
    outbound = pl.pallas_call(
        split_kernel,
        grid_spec=pltpu.PrefetchScalarGridSpec(
            num_scalar_prefetch=1,
            grid=(2,),
            in_specs=[pl.BlockSpec((part, rows, width), lambda a, core: (core[0] * 2 + a, 0, 0))],
            out_specs=pl.BlockSpec((X, rows, 384), lambda a, core: (0, 0, a)),
        ),
        out_shape=jax.ShapeDtypeStruct((X, rows, 768), BF16),
        compiler_params=params(),
        cost_estimate=cost(0, 4 * rows * 768 * 4),
        name="split",
    )(core, features)
    own = lax.all_to_all(outbound, "dp", 0, 0, axis_index_groups=along_x, tiled=True)
    other = lax.ppermute(own, "mp", [(k, k ^ 1) for k in range(heads)])

    step = 4
    attention, grads = pl.pallas_call(
        attend_kernel,
        grid=(heads // step,),
        in_specs=[
            pl.BlockSpec((step, rows, width), lambda k: (k, 0, 0)),
            pl.BlockSpec((step, width, cols), lambda k: (k, 0, 0)),
            pl.BlockSpec((slots, HD), lambda k: (0, 0)),
            pl.BlockSpec((8, 128), lambda k: (0, 0)),
        ],
        out_specs=(
            pl.BlockSpec((slots, HD), lambda k: (0, 0)),
            pl.BlockSpec((rows, cols), lambda k: (0, 0)),
        ),
        out_shape=(
            jax.ShapeDtypeStruct((slots, HD), BF16),
            jax.ShapeDtypeStruct((rows, cols), BF16),
        ),
        scratch_shapes=[pltpu.VMEM((rows, cols), F32)],
        compiler_params=params(),
        cost_estimate=cost(2 * heads * rows * width * cols, 9 * 1024 * 1024),
        name="attend",
    )(features, project_weight.reshape(heads, width, cols), cotangent, offsets)

    all_grads = lax.all_gather(grads, "dp", axis=0, axis_index_groups=along_x)
    terms = pl.pallas_call(
        weight_kernel,
        out_shape=jax.ShapeDtypeStruct((Y, 192, cols), BF16),
        in_specs=[SMEM] + [VMEM] * 3,
        out_specs=VMEM,
        compiler_params=params(),
        cost_estimate=cost(2 * 4 * rows * 1536 * cols, 6 * 1024 * 1024),
        name="weight",
    )(core, own, other, all_grads)
    gathered = lax.all_to_all(terms, "dp", 0, 0, axis_index_groups=along_y, tiled=True)
    weight_grad = pl.pallas_call(
        sum_kernel,
        out_shape=jax.ShapeDtypeStruct((192, cols), F32),
        in_specs=[SMEM, VMEM],
        out_specs=VMEM,
        compiler_params=params(),
        name="sum",
    )(odd, gathered)
    return attention, weight_grad


def solution(mesh):
    in_specs = (P("dp", "mp"), P("dp", None), P("dp", None), P(None, "mp"), P("dp", "mp"))
    out_specs = (P("dp", "mp"), P("dp", "mp"))
    return jax.shard_map(shards, mesh=mesh, in_specs=in_specs, out_specs=out_specs, check_vma=False)
```

```python
import jax
import jax.numpy as jnp
from jax import lax
from jax.experimental import pallas as pl
from jax.experimental.pallas import tpu as pltpu
from jax.sharding import PartitionSpec as P

CAP = 96
HD = 128
SENT = 18
ROOM = 24
X, Y = 4, 8
F32, BF16, I32 = jnp.float32, jnp.bfloat16, jnp.int32


def iota(shape, dim):
    return lax.broadcasted_iota(I32, shape, dim)


def hot(condition):
    return jnp.where(condition, 1.0, 0.0).astype(BF16)


def mm(a, b, ca=1, cb=0):
    return lax.dot_general(a, b, (((ca,), (cb,)), ((), ())), preferred_element_type=F32)


def send_kernel(patches, route, slot, out):
    rows = patches.shape[0]
    owners = out.shape[0] // ROOM
    pack = route[...]
    place = slot[...]
    matches = hot(pack == iota((rows, owners), 1))
    before = mm(hot(iota((rows, rows), 0) > iota((rows, rows), 1)), matches)
    position = jnp.sum(before * matches.astype(F32), axis=1, keepdims=True).astype(I32)
    spread = hot(pack * ROOM + position == iota((rows, owners * ROOM), 1))
    total = mm(spread, patches[...], 0, 0)
    held = hot(position == iota((rows, 256), 1)).astype(F32)
    high = (held * ((place >> 1) + 1).astype(F32)).astype(BF16)
    low = (held * (place & 1).astype(F32)).astype(BF16)
    line, owner = iota((owners * ROOM, owners), 0), iota((owners * ROOM, owners), 1)
    for row, part in ((SENT, high), (SENT + 1, low)):
        total += mm(hot(line == owner * ROOM + row), mm(matches, part, 0, 0).astype(BF16))
    out[...] = total.astype(BF16)


def receive_kernel(arrived, first, second, offsets):
    lines = arrived.shape[0]
    owners = lines // ROOM
    half = first.shape[0]
    rows = 2 * half
    data = arrived[...]
    line, owner = iota((owners, lines), 1), iota((owners, lines), 0)
    spread = hot((line >= owner * ROOM) & (line < owner * ROOM + ROOM))
    within = jnp.sum(
        jnp.where((line >= owner * ROOM) & (line < owner * ROOM + ROOM), line - owner * ROOM, 0),
        axis=0,
        keepdims=True,
    )
    chosen = iota((128, lines), 0) == within
    number = []
    for row in (SENT, SENT + 1):
        part = mm(hot(line == owner * ROOM + row), data)[:, :128].astype(BF16)
        wide = mm(part, spread, 0, 0)
        number.append(jnp.sum(jnp.where(chosen, wide, 0.0), axis=0, keepdims=True).astype(I32))
    live = (number[0] > 0) & (within < SENT)
    place = 2 * (number[0] - 1) + number[1]
    image = sum((place >= CAP * j).astype(I32) for j in (1, 2, 3))
    start, starts, base = jnp.zeros((1, 1), I32), [], jnp.zeros_like(place)
    for j in range(3):
        count = jnp.sum(jnp.where(live & (image == j), 1.0, 0.0), axis=1, keepdims=True)
        start = start + count.astype(I32)
        starts.append(start)
        base = jnp.where(image == j + 1, start, base)
    target = jnp.where(live, base + place - CAP * image, -1)
    both = mm(hot(iota((rows, lines), 0) == target), data).astype(BF16)
    first[...] = both[:half]
    second[...] = both[half:]
    lane = iota((8, 128), 1)
    offsets[...] = sum(jnp.where(lane == j, starts[j], 0) for j in range(3))


def places(index, offsets):
    image, base, last = 0, 0, 0
    for j in range(3):
        start = offsets[0:1, j : j + 1]
        past = index >= start
        image = image + past.astype(I32)
        base = base + jnp.where(past, start - last, 0)
        last = start
    return image, index - base + CAP * image


def attend_kernel(
    core, own1, own2, far1, far2, weight, cotangent, offsets, attention, grads, total
):
    step = pl.program_id(0)
    half = own1.shape[1]
    parts = [None, None]
    for k in range(own1.shape[0]):
        near_weight, far_weight = weight[k, core[0]], weight[k, 1 - core[0]]
        for i, (near, far) in enumerate(((own1, far1), (own2, far2))):
            term = mm(near[k], near_weight) + mm(far[k], far_weight)
            parts[i] = term if k == 0 else parts[i] + term

    @pl.when(step == 0)
    def _():
        total[:half] = parts[0]
        total[half:] = parts[1]

    @pl.when(step > 0)
    def _():
        total[:half] += parts[0]
        total[half:] += parts[1]

    @pl.when(step == pl.num_programs(0) - 1)
    def _():
        rows, slots = total.shape[0], attention.shape[0]
        offs = offsets[...]
        image_col, slot_col = places(iota((rows, 1), 0), offs)
        image_row, slot_row = places(iota((1, rows), 1), offs)
        same = image_col == image_row
        cot = mm(hot(slot_col == iota((rows, slots), 1)), cotangent[...]).astype(BF16)
        rounded = total[...].astype(BF16)
        query, key, value = rounded[:, :HD], rounded[:, HD : 2 * HD], rounded[:, 2 * HD :]
        scale = HD ** (-0.5)
        scores = mm(query, key, 1, 1) * scale
        expscore = jnp.where(same, jnp.exp(jnp.where(same, scores, 0.0)), 0.0)
        softmax = expscore / jnp.sum(expscore, axis=1, keepdims=True)
        weights = softmax.astype(BF16)
        result = mm(weights, value).astype(BF16)
        attention[...] = mm(hot(iota((slots, rows), 0) == slot_row), result).astype(BF16)
        d_value = mm(weights, cot, 0, 0)
        d_weights = mm(cot, value, 1, 1).astype(BF16).astype(F32)
        d_weights = jnp.where(same, d_weights, 0.0)
        inner = jnp.sum(d_weights * softmax, axis=1, keepdims=True)
        d_scores = (softmax * (d_weights - inner) * scale).astype(BF16)
        grads[:, :HD] = mm(d_scores, key).astype(BF16)
        grads[:, HD : 2 * HD] = mm(d_scores, query, 0, 0).astype(BF16)
        grads[:, 2 * HD :] = d_value.astype(BF16)


PICKS = (((0, 1), (4, 1), (5, 2), (3, 2)), ((2, 3), (0, 3), (1, 4), (5, 4)))


def split_kernel(core, features, out):
    row, col = iota((256, 128), 0), iota((256, 128), 1)
    low = hot(row == jnp.where(col < 64, col, col + 64))
    high = hot(row == jnp.where(col < 64, col + 64, col + 128))

    def tile(group, t):
        return features[3 * group + t // 2, :, (t % 2) * 128 : (t % 2) * 128 + 128]

    for side, picks in enumerate(PICKS):

        @pl.when(core[0] == side)
        def _(picks=picks):
            for x, (whole, cut) in enumerate(picks):
                for a in range(2):
                    at = a * 384
                    out[x, :, at : at + 128] = tile(2 * a, whole)
                    out[x, :, at + 128 : at + 256] = tile(2 * a + 1, whole)
                    both = jnp.concatenate([tile(2 * a, cut), tile(2 * a + 1, cut)], axis=1)
                    out[x, :, at + 256 : at + 384] = mm(both, (low, high)[x % 2]).astype(BF16)


def weight_kernel(core, inner, own1, own2, far1, far2, grads, out):
    packs, half = own1.shape[0], own1.shape[1]
    depth = packs * half
    right1 = grads[:, :half].reshape(depth, grads.shape[2])
    right2 = grads[:, half:].reshape(depth, grads.shape[2])
    for left1, left2, side in ((own1, own2, core[0]), (far1, far2, 1 - core[0])):
        whole_side = jnp.where(inner[0] == 1, 1 - side, side)
        for a in range(2):
            at = slice(a * 384, a * 384 + 384)
            term = mm(left1[:, :, at].reshape(depth, 384), right1, 0, 0)
            term += mm(left2[:, :, at].reshape(depth, 384), right2, 0, 0)
            term = term.astype(BF16)
            for b in range(2):
                group = 2 * a + b
                out[2 * group + whole_side, 0:128] = term[b * 128 : b * 128 + 128]
                out[2 * group + side, 128:192] = term[256 + b * 64 : 320 + b * 64]


def sum_kernel(odd, terms, out):
    total = terms[0].astype(F32)
    for k in range(1, terms.shape[0]):
        total += terms[k].astype(F32)

    @pl.when(odd[0] == 0)
    def _():
        out[...] = total

    @pl.when(odd[0] == 1)
    def _():
        out[0:64] = total[128:192]
        out[64:192] = total[0:128]


def params():
    return pltpu.CompilerParams(vmem_limit_bytes=40 * 1024 * 1024)


def cost(flops, moved):
    return pl.CostEstimate(flops=flops, bytes_accessed=moved, transcendentals=0)


VMEM = pl.BlockSpec(memory_space=pltpu.VMEM)
SMEM = pl.BlockSpec(memory_space=pltpu.SMEM)


def shards(patches, pack_route, pack_slot, project_weight, cotangent):
    owners, heads = lax.axis_size("dp"), lax.axis_size("mp")
    rows, width = patches.shape
    slots = cotangent.shape[0]
    cols = project_weight.shape[1]
    core = (lax.axis_index("mp") % 2).astype(I32).reshape(1)
    x_index = lax.axis_index("dp") % X
    inner = ((x_index == 1) | (x_index == 2)).astype(I32).reshape(1)
    odd = (lax.axis_index("dp") % 2).astype(I32).reshape(1)
    along_x = [[y * X + x for x in range(X)] for y in range(Y)]
    along_y = [[y * X + x for y in range(Y)] for x in range(X)]

    outgoing = pl.pallas_call(
        send_kernel,
        out_shape=jax.ShapeDtypeStruct((owners * ROOM, width), BF16),
        in_specs=[VMEM] * 3,
        out_specs=VMEM,
        compiler_params=params(),
        name="send",
    )(patches, pack_route, pack_slot)
    arrived = lax.all_to_all(outgoing.reshape(owners, ROOM, width), "dp", 0, 0, tiled=True)
    half = rows // 2
    first, second, offsets = pl.pallas_call(
        receive_kernel,
        out_shape=(
            jax.ShapeDtypeStruct((half, width), BF16),
            jax.ShapeDtypeStruct((half, width), BF16),
            jax.ShapeDtypeStruct((8, 128), I32),
        ),
        in_specs=[VMEM],
        out_specs=(VMEM, VMEM, VMEM),
        compiler_params=params(),
        name="receive",
    )(arrived.reshape(owners * ROOM, width))

    depth = heads // 2
    same_core = [[2 * z + c for z in range(depth)] for c in range(2)]
    sibling = [(k, k ^ 1) for k in range(heads)]

    def split(features):
        return pl.pallas_call(
            split_kernel,
            out_shape=jax.ShapeDtypeStruct((X, half, 768), BF16),
            in_specs=[SMEM, VMEM],
            out_specs=VMEM,
            compiler_params=params(),
            cost_estimate=cost(0, 2 * half * 768 * 4),
            name="split",
        )(core, features)

    def over_x(block):
        return lax.all_to_all(block, "dp", 0, 0, axis_index_groups=along_x, tiled=True)

    own1 = lax.all_gather(first, "mp", axis=0, axis_index_groups=same_core)
    out1 = split(own1)
    second, out1 = lax.optimization_barrier((second, out1))
    near1 = over_x(out1)
    far1 = lax.ppermute(own1, "mp", sibling)
    own2 = lax.all_gather(second, "mp", axis=0, axis_index_groups=same_core)
    out2 = split(own2)
    near2 = over_x(out2)
    far2 = lax.ppermute(own2, "mp", sibling)

    step = 2
    block = pl.BlockSpec((step, half, width), lambda k, core: (k, 0, 0))
    attention, grads = pl.pallas_call(
        attend_kernel,
        grid_spec=pltpu.PrefetchScalarGridSpec(
            num_scalar_prefetch=1,
            grid=(depth // step,),
            in_specs=[block] * 4
            + [
                pl.BlockSpec((step, 2, width, cols), lambda k, core: (k, 0, 0, 0)),
                pl.BlockSpec((slots, HD), lambda k, core: (0, 0)),
                pl.BlockSpec((8, 128), lambda k, core: (0, 0)),
            ],
            out_specs=(
                pl.BlockSpec((slots, HD), lambda k, core: (0, 0)),
                pl.BlockSpec((rows, cols), lambda k, core: (0, 0)),
            ),
            scratch_shapes=[pltpu.VMEM((rows, cols), F32)],
        ),
        out_shape=(
            jax.ShapeDtypeStruct((slots, HD), BF16),
            jax.ShapeDtypeStruct((rows, cols), BF16),
        ),
        compiler_params=params(),
        cost_estimate=cost(2 * heads * rows * width * cols, 9 * 1024 * 1024),
        name="attend",
    )(
        core, own1, own2, far1, far2,
        project_weight.reshape(depth, 2, width, cols), cotangent, offsets,
    )

    cross1 = lax.ppermute(near1, "mp", sibling)
    near2, grads = lax.optimization_barrier((near2, grads))
    cross2 = lax.ppermute(near2, "mp", sibling)
    all_grads = lax.all_gather(grads, "dp", axis=0, axis_index_groups=along_x)
    terms = pl.pallas_call(
        weight_kernel,
        out_shape=jax.ShapeDtypeStruct((Y, 192, cols), BF16),
        in_specs=[SMEM] * 2 + [VMEM] * 5,
        out_specs=VMEM,
        compiler_params=params(),
        cost_estimate=cost(2 * 4 * rows * 1536 * cols, 6 * 1024 * 1024),
        name="weight",
    )(core, inner, near1, near2, cross1, cross2, all_grads)
    gathered = lax.all_to_all(terms, "dp", 0, 0, axis_index_groups=along_y, tiled=True)
    weight_grad = pl.pallas_call(
        sum_kernel,
        out_shape=jax.ShapeDtypeStruct((192, cols), F32),
        in_specs=[SMEM, VMEM],
        out_specs=VMEM,
        compiler_params=params(),
        name="sum",
    )(odd, gathered)
    return attention, weight_grad


def solution(mesh):
    in_specs = (P("dp", "mp"), P("dp", None), P("dp", None), P(None, "mp"), P("dp", "mp"))
    out_specs = (P("dp", "mp"), P("dp", "mp"))
    return jax.shard_map(shards, mesh=mesh, in_specs=in_specs, out_specs=out_specs, check_vma=False)
```

```python
import jax
import jax.numpy as jnp
from jax import lax
from jax.experimental import pallas as pl
from jax.experimental.pallas import tpu as pltpu
from jax.sharding import PartitionSpec as P

CAP = 96
HD = 128
SENT = 18
ROOM = 24
X, Y = 4, 8
ATTEND_VMEM = 40
F32, BF16, I32 = jnp.float32, jnp.bfloat16, jnp.int32


def iota(shape, dim):
    return lax.broadcasted_iota(I32, shape, dim)


def hot(condition):
    return jnp.where(condition, 1.0, 0.0).astype(BF16)


def mm(a, b, ca=1, cb=0):
    return lax.dot_general(a, b, (((ca,), (cb,)), ((), ())), preferred_element_type=F32)


def send_kernel(patches, route, slot, out):
    rows = patches.shape[0]
    owners = out.shape[0] // ROOM
    pack = route[...]
    place = slot[...]
    matches = hot(pack == iota((rows, owners), 1))
    before = mm(hot(iota((rows, rows), 0) > iota((rows, rows), 1)), matches)
    position = jnp.sum(before * matches.astype(F32), axis=1, keepdims=True).astype(I32)
    spread = hot(pack * ROOM + position == iota((rows, owners * ROOM), 1))
    total = mm(spread, patches[...], 0, 0)
    held = hot(position == iota((rows, 256), 1)).astype(F32)
    high = (held * ((place >> 1) + 1).astype(F32)).astype(BF16)
    low = (held * (place & 1).astype(F32)).astype(BF16)
    line, owner = iota((owners * ROOM, owners), 0), iota((owners * ROOM, owners), 1)
    for row, part in ((SENT, high), (SENT + 1, low)):
        total += mm(hot(line == owner * ROOM + row), mm(matches, part, 0, 0).astype(BF16))
    out[...] = total.astype(BF16)


def receive_kernel(arrived, out, offsets):
    lines = arrived.shape[0]
    owners = lines // ROOM
    rows = out.shape[0]
    data = arrived[...]
    line, owner = iota((owners, lines), 1), iota((owners, lines), 0)
    spread = hot((line >= owner * ROOM) & (line < owner * ROOM + ROOM))
    within = jnp.sum(
        jnp.where((line >= owner * ROOM) & (line < owner * ROOM + ROOM), line - owner * ROOM, 0),
        axis=0,
        keepdims=True,
    )
    chosen = iota((128, lines), 0) == within
    number = []
    for row in (SENT, SENT + 1):
        part = mm(hot(line == owner * ROOM + row), data)[:, :128].astype(BF16)
        wide = mm(part, spread, 0, 0)
        number.append(jnp.sum(jnp.where(chosen, wide, 0.0), axis=0, keepdims=True).astype(I32))
    live = (number[0] > 0) & (within < SENT)
    place = 2 * (number[0] - 1) + number[1]
    image = sum((place >= CAP * j).astype(I32) for j in (1, 2, 3))
    start, starts, base = jnp.zeros((1, 1), I32), [], jnp.zeros_like(place)
    for j in range(3):
        count = jnp.sum(jnp.where(live & (image == j), 1.0, 0.0), axis=1, keepdims=True)
        start = start + count.astype(I32)
        starts.append(start)
        base = jnp.where(image == j + 1, start, base)
    target = jnp.where(live, base + place - CAP * image, -1)
    out[...] = mm(hot(iota((rows, lines), 0) == target), data).astype(BF16)
    lane = iota((8, 128), 1)
    offsets[...] = sum(jnp.where(lane == j, starts[j], 0) for j in range(3))


def places(index, offsets):
    image, base, last = 0, 0, 0
    for j in range(3):
        start = offsets[0:1, j : j + 1]
        past = index >= start
        image = image + past.astype(I32)
        base = base + jnp.where(past, start - last, 0)
        last = start
    return image, index - base + CAP * image


def attend_kernel(
    where, base, up, down, far, far_up, far_down, weight, cotangent, offsets, attention, grads, total
):
    step = pl.program_id(0)
    core = where[0]
    part = mm(base[0], weight[0, where[1], core]) + mm(far[0], weight[0, where[1], 1 - core])
    part += mm(up[0], weight[0, where[2], core]) + mm(far_up[0], weight[0, where[2], 1 - core])
    part += mm(down[0], weight[0, where[3], core]) + mm(far_down[0], weight[0, where[3], 1 - core])

    @pl.when(step == 0)
    def _():
        total[...] = part

    @pl.when(step > 0)
    def _():
        total[...] += part

    @pl.when(step == pl.num_programs(0) - 1)
    def _():
        rows, slots = total.shape[0], attention.shape[0]
        offs = offsets[...]
        image_col, slot_col = places(iota((rows, 1), 0), offs)
        image_row, slot_row = places(iota((1, rows), 1), offs)
        same = image_col == image_row
        cot = mm(hot(slot_col == iota((rows, slots), 1)), cotangent[...]).astype(BF16)
        rounded = total[...].astype(BF16)
        query, key, value = rounded[:, :HD], rounded[:, HD : 2 * HD], rounded[:, 2 * HD :]
        scale = HD ** (-0.5)
        scores = mm(query, key, 1, 1) * scale
        expscore = jnp.where(same, jnp.exp(jnp.where(same, scores, 0.0)), 0.0)
        softmax = expscore / jnp.sum(expscore, axis=1, keepdims=True)
        weights = softmax.astype(BF16)
        result = mm(weights, value).astype(BF16)
        attention[...] = mm(hot(iota((slots, rows), 0) == slot_row), result).astype(BF16)
        d_value = mm(weights, cot, 0, 0)
        d_weights = mm(cot, value, 1, 1).astype(BF16).astype(F32)
        d_weights = jnp.where(same, d_weights, 0.0)
        inner = jnp.sum(d_weights * softmax, axis=1, keepdims=True)
        d_scores = (softmax * (d_weights - inner) * scale).astype(BF16)
        grads[:, :HD] = mm(d_scores, key).astype(BF16)
        grads[:, HD : 2 * HD] = mm(d_scores, query, 0, 0).astype(BF16)
        grads[:, 2 * HD :] = d_value.astype(BF16)


def split_kernel(*refs):
    out = refs[-1]
    row, col = iota((256, 512), 0), iota((256, 512), 1)
    source = ((col >> 4) & 3) * 64 + (col >> 7) * 16 + (col & 15)
    left = hot((row == source) & ((col & 64) == 0))
    right = hot((row == source) & ((col & 64) == 64))
    at = 0
    for features in refs[:-1]:
        for m in range(0, features.shape[0], 2):
            both = (mm(features[m], left) + mm(features[m + 1], right)).astype(BF16)
            for x in range(X):
                out[x, :, at : at + 128] = both[:, x * 128 : x * 128 + 128]
            at += 128


def weight_kernel(where, near1, near2, cross1, cross2, grads, out):
    depth = grads.shape[0] * grads.shape[1]
    right = grads[...].reshape(depth, grads.shape[2])
    core = where[0]
    for first, second, side in ((near1, near2, core), (cross1, cross2, 1 - core)):
        for held, at, turn in ((first, 0, where[1]), (second, 0, where[2]), (second, 256, where[3])):
            left = held[:, :, at : at + 256].reshape(depth, 256)
            term = mm(left, right, 0, 0).astype(BF16)
            for m in range(4):
                slice_index = 6 * m + 2 * turn + side
                rows = pl.ds(pl.multiple_of(slice_index * 64, 64), 64)
                out[rows, :] = term[m * 64 : m * 64 + 64]


def sum_kernel(terms, out):
    for x in range(X):
        total = terms[x].astype(F32)
        for k in range(X + x, terms.shape[0], X):
            total += terms[k].astype(F32)
        for v in range(3):
            out[64 * v + 16 * x : 64 * v + 16 * x + 16] = total[16 * v : 16 * v + 16]


def params():
    return pltpu.CompilerParams(vmem_limit_bytes=40 * 1024 * 1024)


def cost(flops, moved):
    return pl.CostEstimate(flops=flops, bytes_accessed=moved, transcendentals=0)


VMEM = pl.BlockSpec(memory_space=pltpu.VMEM)
SMEM = pl.BlockSpec(memory_space=pltpu.SMEM)


def shards(patches, pack_route, pack_slot, project_weight, cotangent):
    owners, heads = lax.axis_size("dp"), lax.axis_size("mp")
    rows, width = patches.shape
    slots = cotangent.shape[0]
    cols = project_weight.shape[1]
    place = lax.axis_index("mp")
    turn = (place // 2) % 3
    where = jnp.stack([place % 2, turn, (turn + 2) % 3, (turn + 1) % 3]).astype(I32)
    along_x = [[y * X + x for x in range(X)] for y in range(Y)]

    outgoing = pl.pallas_call(
        send_kernel,
        out_shape=jax.ShapeDtypeStruct((owners * ROOM, width), BF16),
        in_specs=[VMEM] * 3,
        out_specs=VMEM,
        compiler_params=params(),
        name="send",
    )(patches, pack_route, pack_slot)
    arrived = lax.all_to_all(outgoing.reshape(owners, ROOM, width), "dp", 0, 0, tiled=True)
    compact, offsets = pl.pallas_call(
        receive_kernel,
        out_shape=(
            jax.ShapeDtypeStruct((rows, width), BF16),
            jax.ShapeDtypeStruct((8, 128), I32),
        ),
        in_specs=[VMEM],
        out_specs=(VMEM, VMEM),
        compiler_params=params(),
        name="receive",
    )(arrived.reshape(owners * ROOM, width))

    thirds = [[6 * m + r for m in range(heads // 6)] for r in range(6)]

    def shift(block, by):
        return lax.ppermute(block, "mp", [(k, (k + by) % heads) for k in range(heads)])

    def swap(block):
        return lax.ppermute(block, "mp", [(k, k ^ 1) for k in range(heads)])

    def split(*blocks):
        wide = 64 * sum(block.shape[0] for block in blocks)
        return pl.pallas_call(
            split_kernel,
            out_shape=jax.ShapeDtypeStruct((X, rows, wide), BF16),
            in_specs=[VMEM] * len(blocks),
            out_specs=VMEM,
            compiler_params=params(),
            cost_estimate=cost(0, 4 * rows * wide * 4),
            name="split",
        )(*blocks)

    def over_x(block):
        return lax.all_to_all(block, "dp", 0, 0, axis_index_groups=along_x, tiled=True)

    base = lax.all_gather(compact, "mp", axis=0, axis_index_groups=thirds)
    up, down, far = shift(base, 2), shift(base, -2), swap(base)
    near1 = over_x(split(base))
    far_up, far_down = swap(up), swap(down)
    near2 = over_x(split(up, down))
    near1, far_down = lax.optimization_barrier((near1, far_down))
    cross1 = swap(near1)

    steps = heads // 6
    block = pl.BlockSpec((1, rows, width), lambda k, where: (k, 0, 0))
    attention, grads = pl.pallas_call(
        attend_kernel,
        grid_spec=pltpu.PrefetchScalarGridSpec(
            num_scalar_prefetch=1,
            grid=(steps,),
            in_specs=[block] * 6
            + [
                pl.BlockSpec((1, 3, 2, width, cols), lambda k, where: (k, 0, 0, 0, 0)),
                pl.BlockSpec((slots, HD), lambda k, where: (0, 0)),
                pl.BlockSpec((8, 128), lambda k, where: (0, 0)),
            ],
            out_specs=(
                pl.BlockSpec((slots, HD), lambda k, where: (0, 0)),
                pl.BlockSpec((rows, cols), lambda k, where: (0, 0)),
            ),
            scratch_shapes=[pltpu.VMEM((rows, cols), F32)],
        ),
        out_shape=(
            jax.ShapeDtypeStruct((slots, HD), BF16),
            jax.ShapeDtypeStruct((rows, cols), BF16),
        ),
        compiler_params=pltpu.CompilerParams(vmem_limit_bytes=ATTEND_VMEM * 1024 * 1024),
        cost_estimate=cost(2 * heads * rows * width * cols, 9 * 1024 * 1024),
        name="attend",
    )(
        where, base, up, down, far, far_up, far_down,
        project_weight.reshape(steps, 3, 2, width, cols), cotangent, offsets,
    )

    grads, cross1 = lax.optimization_barrier((grads, cross1))
    all_grads = lax.all_gather(grads, "dp", axis=0, axis_index_groups=along_x)
    near2, all_grads = lax.optimization_barrier((near2, all_grads))
    cross2 = swap(near2)
    terms = pl.pallas_call(
        weight_kernel,
        out_shape=jax.ShapeDtypeStruct((1536, cols), BF16),
        in_specs=[SMEM] + [VMEM] * 5,
        out_specs=VMEM,
        compiler_params=params(),
        cost_estimate=cost(2 * 4 * rows * 1536 * cols, 6 * 1024 * 1024),
        name="weight",
    )(where, near1, near2, cross1, cross2, all_grads)
    gathered = lax.all_to_all(terms.reshape(owners, 48, cols), "dp", 0, 0, tiled=True)
    weight_grad = pl.pallas_call(
        sum_kernel,
        out_shape=jax.ShapeDtypeStruct((192, cols), F32),
        in_specs=[VMEM],
        out_specs=VMEM,
        compiler_params=params(),
        name="sum",
    )(gathered)
    return attention, weight_grad


def solution(mesh):
    in_specs = (P("dp", "mp"), P("dp", None), P("dp", None), P(None, "mp"), P("dp", "mp"))
    out_specs = (P("dp", "mp"), P("dp", "mp"))
    return jax.shard_map(shards, mesh=mesh, in_specs=in_specs, out_specs=out_specs, check_vma=False)
```

```python
import jax
import jax.numpy as jnp
from jax import lax
from jax.experimental import pallas as pl
from jax.experimental.pallas import tpu as pltpu
from jax.sharding import PartitionSpec as P

CAP = 96
HD = 128
SENT = 18
ROOM = 24
X, Y = 4, 8
ATTEND_VMEM = 48
F32, BF16, I32 = jnp.float32, jnp.bfloat16, jnp.int32


def iota(shape, dim):
    return lax.broadcasted_iota(I32, shape, dim)


def hot(condition):
    return jnp.where(condition, 1.0, 0.0).astype(BF16)


def mm(a, b, ca=1, cb=0):
    return lax.dot_general(a, b, (((ca,), (cb,)), ((), ())), preferred_element_type=F32)


def send_kernel(patches, route, slot, out):
    rows = patches.shape[0]
    owners = out.shape[0] // ROOM
    pack = route[...]
    place = slot[...]
    matches = hot(pack == iota((rows, owners), 1))
    before = mm(hot(iota((rows, rows), 0) > iota((rows, rows), 1)), matches)
    position = jnp.sum(before * matches.astype(F32), axis=1, keepdims=True).astype(I32)
    spread = hot(pack * ROOM + position == iota((rows, owners * ROOM), 1))
    total = mm(spread, patches[...], 0, 0)
    held = hot(position == iota((rows, 256), 1)).astype(F32)
    high = (held * ((place >> 1) + 1).astype(F32)).astype(BF16)
    low = (held * (place & 1).astype(F32)).astype(BF16)
    line, owner = iota((owners * ROOM, owners), 0), iota((owners * ROOM, owners), 1)
    for row, part in ((SENT, high), (SENT + 1, low)):
        total += mm(hot(line == owner * ROOM + row), mm(matches, part, 0, 0).astype(BF16))
    out[...] = total.astype(BF16)


def receive_kernel(arrived, out, offsets):
    lines = arrived.shape[0]
    owners = lines // ROOM
    rows = out.shape[0]
    data = arrived[...]
    line, owner = iota((owners, lines), 1), iota((owners, lines), 0)
    spread = hot((line >= owner * ROOM) & (line < owner * ROOM + ROOM))
    within = jnp.sum(
        jnp.where((line >= owner * ROOM) & (line < owner * ROOM + ROOM), line - owner * ROOM, 0),
        axis=0,
        keepdims=True,
    )
    chosen = iota((128, lines), 0) == within
    number = []
    for row in (SENT, SENT + 1):
        part = mm(hot(line == owner * ROOM + row), data)[:, :128].astype(BF16)
        wide = mm(part, spread, 0, 0)
        number.append(jnp.sum(jnp.where(chosen, wide, 0.0), axis=0, keepdims=True).astype(I32))
    live = (number[0] > 0) & (within < SENT)
    place = 2 * (number[0] - 1) + number[1]
    image = sum((place >= CAP * j).astype(I32) for j in (1, 2, 3))
    start, starts, base = jnp.zeros((1, 1), I32), [], jnp.zeros_like(place)
    for j in range(3):
        count = jnp.sum(jnp.where(live & (image == j), 1.0, 0.0), axis=1, keepdims=True)
        start = start + count.astype(I32)
        starts.append(start)
        base = jnp.where(image == j + 1, start, base)
    target = jnp.where(live, base + place - CAP * image, -1)
    out[...] = mm(hot(iota((rows, lines), 0) == target), data).astype(BF16)
    lane = iota((8, 128), 1)
    offsets[...] = sum(jnp.where(lane == j, starts[j], 0) for j in range(3))


def places(index, offsets):
    image, base, last = 0, 0, 0
    for j in range(3):
        start = offsets[0:1, j : j + 1]
        past = index >= start
        image = image + past.astype(I32)
        base = base + jnp.where(past, start - last, 0)
        last = start
    return image, index - base + CAP * image


def attend_kernel(
    where, base, up, down, far, far_up, far_down, weight, cotangent, offsets, attention, grads, total
):
    step = pl.program_id(0)
    core = where[0]
    part = mm(base[0], weight[0, where[1], core]) + mm(far[0], weight[0, where[1], 1 - core])
    part += mm(up[0], weight[0, where[2], core]) + mm(far_up[0], weight[0, where[2], 1 - core])
    part += mm(down[0], weight[0, where[3], core]) + mm(far_down[0], weight[0, where[3], 1 - core])

    @pl.when(step == 0)
    def _():
        total[...] = part

    @pl.when(step > 0)
    def _():
        total[...] += part

    @pl.when(step == pl.num_programs(0) - 1)
    def _():
        rows, slots = total.shape[0], attention.shape[0]
        offs = offsets[...]
        image_col, slot_col = places(iota((rows, 1), 0), offs)
        image_row, slot_row = places(iota((1, rows), 1), offs)
        same = image_col == image_row
        cot = mm(hot(slot_col == iota((rows, slots), 1)), cotangent[...]).astype(BF16)
        rounded = total[...].astype(BF16)
        query, key, value = rounded[:, :HD], rounded[:, HD : 2 * HD], rounded[:, 2 * HD :]
        scale = HD ** (-0.5)
        scores = mm(query, key, 1, 1) * scale
        expscore = jnp.where(same, jnp.exp(jnp.where(same, scores, 0.0)), 0.0)
        softmax = expscore / jnp.sum(expscore, axis=1, keepdims=True)
        weights = softmax.astype(BF16)
        result = mm(weights, value).astype(BF16)
        attention[...] = mm(hot(iota((slots, rows), 0) == slot_row), result).astype(BF16)
        d_value = mm(weights, cot, 0, 0)
        d_weights = mm(cot, value, 1, 1).astype(BF16).astype(F32)
        d_weights = jnp.where(same, d_weights, 0.0)
        inner = jnp.sum(d_weights * softmax, axis=1, keepdims=True)
        d_scores = (softmax * (d_weights - inner) * scale).astype(BF16)
        grads[:, :HD] = mm(d_scores, key).astype(BF16)
        grads[:, HD : 2 * HD] = mm(d_scores, query, 0, 0).astype(BF16)
        grads[:, 2 * HD :] = d_value.astype(BF16)


PICKS = (((0, 1), (4, 1), (5, 2), (3, 2)), ((2, 3), (0, 3), (1, 4), (5, 4)))


def split_kernel(where, base, up, down, out):
    row, col = iota((256, 128), 0), iota((256, 128), 1)
    low = hot(row == jnp.where(col < 64, col, col + 64))
    high = hot(row == jnp.where(col < 64, col + 64, col + 128))

    def spread(picks, held):
        def tile(group, t):
            return held[t // 2][group, :, (t % 2) * 128 : (t % 2) * 128 + 128]

        for x, (whole, cut) in enumerate(picks):
            for a in range(2):
                at = a * 384
                out[x, :, at : at + 128] = tile(2 * a, whole)
                out[x, :, at + 128 : at + 256] = tile(2 * a + 1, whole)
                both = jnp.concatenate([tile(2 * a, cut), tile(2 * a + 1, cut)], axis=1)
                out[x, :, at + 256 : at + 384] = mm(both, (low, high)[x % 2]).astype(BF16)

    for side, picks in enumerate(PICKS):
        for turn, held in enumerate(((base, down, up), (up, base, down), (down, up, base))):

            @pl.when((where[0] == side) & (where[1] == turn))
            def _(picks=picks, held=held):
                spread(picks, held)


def weight_kernel(where, near, cross, grads, out):
    depth = grads.shape[0] * grads.shape[1]
    right = grads[...].reshape(depth, grads.shape[2])
    for held, side in ((near, where[0]), (cross, 1 - where[0])):
        whole_side = jnp.where(where[4] == 1, 1 - side, side)
        for a in range(2):
            left = held[:, :, a * 384 : a * 384 + 384].reshape(depth, 384)
            term = mm(left, right, 0, 0).astype(BF16)
            for b in range(2):
                group = 2 * a + b
                out[2 * group + whole_side, 0:128] = term[b * 128 : b * 128 + 128]
                out[2 * group + side, 128:192] = term[256 + b * 64 : 320 + b * 64]


def sum_kernel(where, terms, out):
    total = terms[0].astype(F32)
    for k in range(1, terms.shape[0]):
        total += terms[k].astype(F32)

    @pl.when(where[5] == 0)
    def _():
        out[...] = total

    @pl.when(where[5] == 1)
    def _():
        out[0:64] = total[128:192]
        out[64:192] = total[0:128]


def params():
    return pltpu.CompilerParams(vmem_limit_bytes=40 * 1024 * 1024)


def cost(flops, moved):
    return pl.CostEstimate(flops=flops, bytes_accessed=moved, transcendentals=0)


VMEM = pl.BlockSpec(memory_space=pltpu.VMEM)
SMEM = pl.BlockSpec(memory_space=pltpu.SMEM)


def shards(patches, pack_route, pack_slot, project_weight, cotangent):
    owners, heads = lax.axis_size("dp"), lax.axis_size("mp")
    rows, width = patches.shape
    slots = cotangent.shape[0]
    cols = project_weight.shape[1]
    place = lax.axis_index("mp")
    turn = (place // 2) % 3
    x_index = lax.axis_index("dp") % X
    inner = (x_index == 1) | (x_index == 2)
    where = [place % 2, turn, (turn + 2) % 3, (turn + 1) % 3, inner, x_index % 2]
    where = jnp.stack([value.astype(I32) for value in where])
    along_x = [[y * X + x for x in range(X)] for y in range(Y)]
    along_y = [[y * X + x for y in range(Y)] for x in range(X)]

    outgoing = pl.pallas_call(
        send_kernel,
        out_shape=jax.ShapeDtypeStruct((owners * ROOM, width), BF16),
        in_specs=[VMEM] * 3,
        out_specs=VMEM,
        compiler_params=params(),
        name="send",
    )(patches, pack_route, pack_slot)
    arrived = lax.all_to_all(outgoing.reshape(owners, ROOM, width), "dp", 0, 0, tiled=True)
    compact, offsets = pl.pallas_call(
        receive_kernel,
        out_shape=(
            jax.ShapeDtypeStruct((rows, width), BF16),
            jax.ShapeDtypeStruct((8, 128), I32),
        ),
        in_specs=[VMEM],
        out_specs=(VMEM, VMEM),
        compiler_params=params(),
        name="receive",
    )(arrived.reshape(owners * ROOM, width))

    thirds = [[6 * m + r for m in range(heads // 6)] for r in range(6)]

    def shift(block, by):
        return lax.ppermute(block, "mp", [(k, (k + by) % heads) for k in range(heads)])

    def swap(block):
        return lax.ppermute(block, "mp", [(k, k ^ 1) for k in range(heads)])

    base = lax.all_gather(compact, "mp", axis=0, axis_index_groups=thirds)
    up, down, far = shift(base, 2), shift(base, -2), swap(base)
    up, down, far = lax.optimization_barrier((up, down, far))
    far_up, far_down = swap(up), swap(down)
    outbound = pl.pallas_call(
        split_kernel,
        out_shape=jax.ShapeDtypeStruct((X, rows, 768), BF16),
        in_specs=[SMEM] + [VMEM] * 3,
        out_specs=VMEM,
        compiler_params=params(),
        cost_estimate=cost(0, 4 * rows * 768 * 4),
        name="split",
    )(where, base, up, down)
    near = lax.all_to_all(outbound, "dp", 0, 0, axis_index_groups=along_x, tiled=True)

    steps = heads // 6
    block = pl.BlockSpec((1, rows, width), lambda k, where: (k, 0, 0))
    attention, grads = pl.pallas_call(
        attend_kernel,
        grid_spec=pltpu.PrefetchScalarGridSpec(
            num_scalar_prefetch=1,
            grid=(steps,),
            in_specs=[block] * 6
            + [
                pl.BlockSpec((1, 3, 2, width, cols), lambda k, where: (k, 0, 0, 0, 0)),
                pl.BlockSpec((slots, HD), lambda k, where: (0, 0)),
                pl.BlockSpec((8, 128), lambda k, where: (0, 0)),
            ],
            out_specs=(
                pl.BlockSpec((slots, HD), lambda k, where: (0, 0)),
                pl.BlockSpec((rows, cols), lambda k, where: (0, 0)),
            ),
            scratch_shapes=[pltpu.VMEM((rows, cols), F32)],
        ),
        out_shape=(
            jax.ShapeDtypeStruct((slots, HD), BF16),
            jax.ShapeDtypeStruct((rows, cols), BF16),
        ),
        compiler_params=pltpu.CompilerParams(vmem_limit_bytes=ATTEND_VMEM * 1024 * 1024),
        cost_estimate=cost(2 * heads * rows * width * cols, 9 * 1024 * 1024),
        name="attend",
    )(
        where, base, up, down, far, far_up, far_down,
        project_weight.reshape(steps, 3, 2, width, cols), cotangent, offsets,
    )

    all_grads = lax.all_gather(grads, "dp", axis=0, axis_index_groups=along_x)
    near, all_grads = lax.optimization_barrier((near, all_grads))
    cross = swap(near)
    terms = pl.pallas_call(
        weight_kernel,
        out_shape=jax.ShapeDtypeStruct((Y, 192, cols), BF16),
        in_specs=[SMEM] + [VMEM] * 3,
        out_specs=VMEM,
        compiler_params=params(),
        cost_estimate=cost(2 * 4 * rows * 1536 * cols, 6 * 1024 * 1024),
        name="weight",
    )(where, near, cross, all_grads)
    gathered = lax.all_to_all(terms, "dp", 0, 0, axis_index_groups=along_y, tiled=True)
    weight_grad = pl.pallas_call(
        sum_kernel,
        out_shape=jax.ShapeDtypeStruct((192, cols), F32),
        in_specs=[SMEM, VMEM],
        out_specs=VMEM,
        compiler_params=params(),
        name="sum",
    )(where, gathered)
    return attention, weight_grad


def solution(mesh):
    in_specs = (P("dp", "mp"), P("dp", None), P("dp", None), P(None, "mp"), P("dp", "mp"))
    out_specs = (P("dp", "mp"), P("dp", "mp"))
    return jax.shard_map(shards, mesh=mesh, in_specs=in_specs, out_specs=out_specs, check_vma=False)
```

```python
import jax
import jax.numpy as jnp
from jax import lax
from jax.experimental import pallas as pl
from jax.experimental.pallas import tpu as pltpu
from jax.sharding import PartitionSpec as P

CAP = 96
HD = 128
SENT = 18
ROOM = 24
X, Y = 4, 8
PROJECT_VMEM = 48
F32, BF16, I32 = jnp.float32, jnp.bfloat16, jnp.int32


def iota(shape, dim):
    return lax.broadcasted_iota(I32, shape, dim)


def hot(condition):
    return jnp.where(condition, 1.0, 0.0).astype(BF16)


def mm(a, b, ca=1, cb=0):
    return lax.dot_general(a, b, (((ca,), (cb,)), ((), ())), preferred_element_type=F32)


def send_kernel(patches_in, route_in, slot_in, out, patches, route, slot, done):
    pairs = ((route_in, route), (slot_in, slot), (patches_in, patches))
    copies = [pltpu.make_async_copy(a, b, done.at[i]) for i, (a, b) in enumerate(pairs)]
    for copy in copies:
        copy.start()
    for copy in copies:
        copy.wait()
    rows = patches.shape[0]
    owners = out.shape[0] // ROOM
    pack = route[...]
    place = slot[...]
    matches = hot(pack == iota((owners, rows), 0))
    before = mm(matches, hot(iota((rows, rows), 0) < iota((rows, rows), 1)))
    matches = matches.astype(F32)
    position = jnp.sum(before * matches, axis=0, keepdims=True).astype(I32)
    total = mm(hot(pack * ROOM + position == iota((owners * ROOM, rows), 0)), patches[...])
    held = hot(position == iota((256, rows), 0))
    high = (matches * ((place >> 1) + 1).astype(F32)).astype(BF16)
    low = (matches * (place & 1).astype(F32)).astype(BF16)
    line, owner = iota((owners * ROOM, owners), 0), iota((owners * ROOM, owners), 1)
    for row, part in ((SENT, high), (SENT + 1, low)):
        total += mm(hot(line == owner * ROOM + row), mm(part, held, 1, 1).astype(BF16))
    out[...] = total.astype(BF16)


def receive_kernel(arrived, out, offsets):
    lines = arrived.shape[0]
    owners = lines // ROOM
    rows = out.shape[0]
    data = arrived[...]
    line, owner = iota((owners, lines), 1), iota((owners, lines), 0)
    spread = hot((line >= owner * ROOM) & (line < owner * ROOM + ROOM))
    within = jnp.sum(
        jnp.where((line >= owner * ROOM) & (line < owner * ROOM + ROOM), line - owner * ROOM, 0),
        axis=0,
        keepdims=True,
    )
    chosen = iota((128, lines), 0) == within
    number = []
    for row in (SENT, SENT + 1):
        part = mm(hot(line == owner * ROOM + row), data)[:, :128].astype(BF16)
        wide = mm(part, spread, 0, 0)
        number.append(jnp.sum(jnp.where(chosen, wide, 0.0), axis=0, keepdims=True).astype(I32))
    live = (number[0] > 0) & (within < SENT)
    place = 2 * (number[0] - 1) + number[1]
    image = sum((place >= CAP * j).astype(I32) for j in (1, 2, 3))
    start, starts, base = jnp.zeros((1, 1), I32), [], jnp.zeros_like(place)
    for j in range(3):
        count = jnp.sum(jnp.where(live & (image == j), 1.0, 0.0), axis=1, keepdims=True)
        start = start + count.astype(I32)
        starts.append(start)
        base = jnp.where(image == j + 1, start, base)
    target = jnp.where(live, base + place - CAP * image, -1)
    out[...] = mm(hot(iota((rows, lines), 0) == target), data).astype(BF16)
    lane = iota((8, 128), 1)
    offsets[...] = sum(jnp.where(lane == j, starts[j], 0) for j in range(3))


def places(index, offsets):
    image, base, last = 0, 0, 0
    for j in range(3):
        start = offsets[0:1, j : j + 1]
        past = index >= start
        image = image + past.astype(I32)
        base = base + jnp.where(past, start - last, 0)
        last = start
    return image, index - base + CAP * image


def project_kernel(where, base, up, down, weight, far_weight, own, far):
    step = pl.program_id(0)
    for block, out in ((weight, own), (far_weight, far)):
        part = mm(base[0], block[0, where[1], 0])
        part += mm(up[0], block[0, where[2], 0])
        part += mm(down[0], block[0, where[3], 0])

        @pl.when(step == 0)
        def _(part=part, out=out):
            out[...] = part

        @pl.when(step > 0)
        def _(part=part, out=out):
            out[...] += part


def attend_kernel(own, far, cotangent, offsets, attention, grads):
    rows, slots = grads.shape[0], attention.shape[0]
    offs = offsets[...]
    image_col, slot_col = places(iota((rows, 1), 0), offs)
    image_row, slot_row = places(iota((1, rows), 1), offs)
    same = image_col == image_row
    cot = mm(hot(slot_col == iota((rows, slots), 1)), cotangent[...]).astype(BF16)
    rounded = (own[...] + far[...]).astype(BF16)
    query, key, value = rounded[:, :HD], rounded[:, HD : 2 * HD], rounded[:, 2 * HD :]
    scale = HD ** (-0.5)
    scores = mm(query, key, 1, 1) * scale
    expscore = jnp.where(same, jnp.exp(jnp.where(same, scores, 0.0)), 0.0)
    softmax = expscore / jnp.sum(expscore, axis=1, keepdims=True)
    weights = softmax.astype(BF16)
    result = mm(weights, value).astype(BF16)
    attention[...] = mm(hot(iota((slots, rows), 0) == slot_row), result).astype(BF16)
    d_value = mm(weights, cot, 0, 0)
    d_weights = mm(cot, value, 1, 1).astype(BF16).astype(F32)
    d_weights = jnp.where(same, d_weights, 0.0)
    inner = jnp.sum(d_weights * softmax, axis=1, keepdims=True)
    d_scores = (softmax * (d_weights - inner) * scale).astype(BF16)
    grads[:, :HD] = mm(d_scores, key).astype(BF16)
    grads[:, HD : 2 * HD] = mm(d_scores, query, 0, 0).astype(BF16)
    grads[:, 2 * HD :] = d_value.astype(BF16)


PICKS = (((0, 1), (4, 1), (5, 2), (3, 2)), ((2, 3), (0, 3), (1, 4), (5, 4)))


def split_kernel(where, base, up, down, out):
    row, col = iota((256, 128), 0), iota((256, 128), 1)
    low = hot(row == jnp.where(col < 64, col, col + 64))
    high = hot(row == jnp.where(col < 64, col + 64, col + 128))

    def spread(picks, held):
        def tile(group, t):
            return held[t // 2][group, :, (t % 2) * 128 : (t % 2) * 128 + 128]

        for x, (whole, cut) in enumerate(picks):
            for a in range(2):
                at = a * 384
                out[x, :, at : at + 128] = tile(2 * a, whole)
                out[x, :, at + 128 : at + 256] = tile(2 * a + 1, whole)
                both = jnp.concatenate([tile(2 * a, cut), tile(2 * a + 1, cut)], axis=1)
                out[x, :, at + 256 : at + 384] = mm(both, (low, high)[x % 2]).astype(BF16)

    for side, picks in enumerate(PICKS):
        for turn, held in enumerate(((base, down, up), (up, base, down), (down, up, base))):

            @pl.when((where[0] == side) & (where[1] == turn))
            def _(picks=picks, held=held):
                spread(picks, held)


def weight_kernel(where, near, cross, grads, out):
    depth = grads.shape[0] * grads.shape[1]
    right = grads[...].reshape(depth, grads.shape[2])
    for held, side in ((near, where[0]), (cross, 1 - where[0])):
        whole_side = jnp.where(where[4] == 1, 1 - side, side)
        for a in range(2):
            left = held[:, :, a * 384 : a * 384 + 384].reshape(depth, 384)
            term = mm(left, right, 0, 0).astype(BF16)
            for b in range(2):
                group = 2 * a + b
                out[2 * group + whole_side, 0:128] = term[b * 128 : b * 128 + 128]
                out[2 * group + side, 128:192] = term[256 + b * 64 : 320 + b * 64]


def sum_kernel(where, terms, out):
    total = terms[0].astype(F32)
    for k in range(1, terms.shape[0]):
        total += terms[k].astype(F32)

    @pl.when(where[5] == 0)
    def _():
        out[...] = total

    @pl.when(where[5] == 1)
    def _():
        out[0:64] = total[128:192]
        out[64:192] = total[0:128]


def params():
    return pltpu.CompilerParams(vmem_limit_bytes=40 * 1024 * 1024)


def cost(flops, moved):
    return pl.CostEstimate(flops=flops, bytes_accessed=moved, transcendentals=0)


VMEM = pl.BlockSpec(memory_space=pltpu.VMEM)
SMEM = pl.BlockSpec(memory_space=pltpu.SMEM)


def shards(patches, pack_route, pack_slot, project_weight, cotangent):
    owners, heads = lax.axis_size("dp"), lax.axis_size("mp")
    rows, width = patches.shape
    slots = cotangent.shape[0]
    cols = project_weight.shape[1]
    place = lax.axis_index("mp")
    turn = (place // 2) % 3
    x_index = lax.axis_index("dp") % X
    inner = (x_index == 1) | (x_index == 2)
    where = [place % 2, turn, (turn + 2) % 3, (turn + 1) % 3, inner, x_index % 2]
    where = jnp.stack([value.astype(I32) for value in where])
    along_x = [[y * X + x for x in range(X)] for y in range(Y)]
    along_y = [[y * X + x for y in range(Y)] for x in range(X)]

    outgoing = pl.pallas_call(
        send_kernel,
        out_shape=jax.ShapeDtypeStruct((owners * ROOM, width), BF16),
        in_specs=[pl.BlockSpec(memory_space=pl.ANY)] * 3,
        out_specs=VMEM,
        scratch_shapes=[
            pltpu.VMEM((rows, width), BF16),
            pltpu.VMEM((1, rows), I32),
            pltpu.VMEM((1, rows), I32),
            pltpu.SemaphoreType.DMA((3,)),
        ],
        compiler_params=params(),
        name="send",
    )(patches, pack_route.reshape(1, rows), pack_slot.reshape(1, rows))
    arrived = lax.all_to_all(outgoing.reshape(owners, ROOM, width), "dp", 0, 0, tiled=True)
    compact, offsets = pl.pallas_call(
        receive_kernel,
        out_shape=(
            jax.ShapeDtypeStruct((rows, width), BF16),
            jax.ShapeDtypeStruct((8, 128), I32),
        ),
        in_specs=[VMEM],
        out_specs=(VMEM, VMEM),
        compiler_params=params(),
        name="receive",
    )(arrived.reshape(owners * ROOM, width))

    thirds = [[6 * m + r for m in range(heads // 6)] for r in range(6)]

    def shift(block, by):
        return lax.ppermute(block, "mp", [(k, (k + by) % heads) for k in range(heads)])

    def swap(block):
        return lax.ppermute(block, "mp", [(k, k ^ 1) for k in range(heads)])

    far_weight = swap(project_weight)
    base = lax.all_gather(compact, "mp", axis=0, axis_index_groups=thirds)
    up, down = shift(base, 2), shift(base, -2)

    steps = heads // 6
    block = pl.BlockSpec((1, rows, width), lambda k, where: (k, 0, 0))
    weight_block = pl.BlockSpec((1, 3, 1, width, cols), lambda k, where: (k, 0, where[0], 0, 0))
    result = pl.BlockSpec((rows, cols), lambda k, where: (0, 0))
    own, far = pl.pallas_call(
        project_kernel,
        grid_spec=pltpu.PrefetchScalarGridSpec(
            num_scalar_prefetch=1,
            grid=(steps,),
            in_specs=[block] * 3 + [weight_block] * 2,
            out_specs=(result, result),
        ),
        out_shape=(jax.ShapeDtypeStruct((rows, cols), F32),) * 2,
        compiler_params=pltpu.CompilerParams(vmem_limit_bytes=PROJECT_VMEM * 1024 * 1024),
        cost_estimate=cost(2 * heads * rows * width * cols, 9 * 1024 * 1024),
        name="project",
    )(
        where, base, up, down,
        project_weight.reshape(steps, 3, 2, width, cols),
        far_weight.reshape(steps, 3, 2, width, cols),
    )
    own_far = swap(far)
    outbound = pl.pallas_call(
        split_kernel,
        out_shape=jax.ShapeDtypeStruct((X, rows, 768), BF16),
        in_specs=[SMEM] + [VMEM] * 3,
        out_specs=VMEM,
        compiler_params=params(),
        cost_estimate=cost(0, 4 * rows * 768 * 4),
        name="split",
    )(where, base, up, down)
    near = lax.all_to_all(outbound, "dp", 0, 0, axis_index_groups=along_x, tiled=True)
    attention, grads = pl.pallas_call(
        attend_kernel,
        out_shape=(
            jax.ShapeDtypeStruct((slots, HD), BF16),
            jax.ShapeDtypeStruct((rows, cols), BF16),
        ),
        in_specs=[VMEM] * 4,
        out_specs=(VMEM, VMEM),
        compiler_params=params(),
        cost_estimate=cost(2 * 9 * rows * rows * HD, 2 * 1024 * 1024),
        name="attend",
    )(own, own_far, cotangent, offsets)

    all_grads = lax.all_gather(grads, "dp", axis=0, axis_index_groups=along_x)
    near, all_grads = lax.optimization_barrier((near, all_grads))
    cross = swap(near)
    terms = pl.pallas_call(
        weight_kernel,
        out_shape=jax.ShapeDtypeStruct((Y, 192, cols), BF16),
        in_specs=[SMEM] + [VMEM] * 3,
        out_specs=VMEM,
        compiler_params=params(),
        cost_estimate=cost(2 * 4 * rows * 1536 * cols, 6 * 1024 * 1024),
        name="weight",
    )(where, near, cross, all_grads)
    gathered = lax.all_to_all(terms, "dp", 0, 0, axis_index_groups=along_y, tiled=True)
    weight_grad = pl.pallas_call(
        sum_kernel,
        out_shape=jax.ShapeDtypeStruct((192, cols), F32),
        in_specs=[SMEM, VMEM],
        out_specs=VMEM,
        compiler_params=params(),
        name="sum",
    )(where, gathered)
    return attention, weight_grad


def solution(mesh):
    in_specs = (P("dp", "mp"), P("dp", None), P("dp", None), P(None, "mp"), P("dp", "mp"))
    out_specs = (P("dp", "mp"), P("dp", "mp"))
    return jax.shard_map(shards, mesh=mesh, in_specs=in_specs, out_specs=out_specs, check_vma=False)
```

```python
import jax
import jax.numpy as jnp
from jax import lax
from jax.experimental import pallas as pl
from jax.experimental.pallas import tpu as pltpu
from jax.sharding import PartitionSpec as P

CAP = 96
HD = 128
SENT = 18
ROOM = 24
X, Y = 4, 8
PROJECT_VMEM = 48
SEND_VMEM = 60
F32, BF16, I32 = jnp.float32, jnp.bfloat16, jnp.int32


def iota(shape, dim):
    return lax.broadcasted_iota(I32, shape, dim)


def hot(condition):
    return jnp.where(condition, 1.0, 0.0).astype(BF16)


def mm(a, b, ca=1, cb=0):
    return lax.dot_general(a, b, (((ca,), (cb,)), ((), ())), preferred_element_type=F32)


def send_kernel(patches_in, route_in, slot_in, out, patches, route, slot, done):
    pairs = ((route_in, route), (slot_in, slot), (patches_in, patches))
    copies = [pltpu.make_async_copy(a, b, done.at[i]) for i, (a, b) in enumerate(pairs)]
    for copy in copies:
        copy.start()
    for copy in copies:
        copy.wait()
    rows = patches.shape[0]
    owners = out.shape[0] // ROOM
    pack = route[...]
    place = slot[...]
    matches = hot(pack == iota((owners, rows), 0))
    before = mm(matches, hot(iota((rows, rows), 0) < iota((rows, rows), 1)))
    matches = matches.astype(F32)
    position = jnp.sum(before * matches, axis=0, keepdims=True).astype(I32)
    total = mm(hot(pack * ROOM + position == iota((owners * ROOM, rows), 0)), patches[...])
    held = hot(position == iota((256, rows), 0))
    high = (matches * ((place >> 1) + 1).astype(F32)).astype(BF16)
    low = (matches * (place & 1).astype(F32)).astype(BF16)
    line, owner = iota((owners * ROOM, owners), 0), iota((owners * ROOM, owners), 1)
    for row, part in ((SENT, high), (SENT + 1, low)):
        total += mm(hot(line == owner * ROOM + row), mm(part, held, 1, 1).astype(BF16))
    out[...] = total.astype(BF16)


def receive_kernel(arrived, out, offsets):
    lines = arrived.shape[0]
    owners = lines // ROOM
    rows = out.shape[0]
    data = arrived[...]
    line, owner = iota((owners, lines), 1), iota((owners, lines), 0)
    spread = hot((line >= owner * ROOM) & (line < owner * ROOM + ROOM))
    within = jnp.sum(
        jnp.where((line >= owner * ROOM) & (line < owner * ROOM + ROOM), line - owner * ROOM, 0),
        axis=0,
        keepdims=True,
    )
    chosen = iota((128, lines), 0) == within
    number = []
    for row in (SENT, SENT + 1):
        part = mm(hot(line == owner * ROOM + row), data)[:, :128].astype(BF16)
        wide = mm(part, spread, 0, 0)
        number.append(jnp.sum(jnp.where(chosen, wide, 0.0), axis=0, keepdims=True).astype(I32))
    live = (number[0] > 0) & (within < SENT)
    place = 2 * (number[0] - 1) + number[1]
    image = sum((place >= CAP * j).astype(I32) for j in (1, 2, 3))
    start, starts, base = jnp.zeros((1, 1), I32), [], jnp.zeros_like(place)
    for j in range(3):
        count = jnp.sum(jnp.where(live & (image == j), 1.0, 0.0), axis=1, keepdims=True)
        start = start + count.astype(I32)
        starts.append(start)
        base = jnp.where(image == j + 1, start, base)
    target = jnp.where(live, base + place - CAP * image, -1)
    out[...] = mm(hot(iota((rows, lines), 0) == target), data).astype(BF16)
    lane = iota((8, 128), 1)
    offsets[...] = sum(jnp.where(lane == j, starts[j], 0) for j in range(3))


def places(index, offsets):
    image, base, last = 0, 0, 0
    for j in range(3):
        start = offsets[0:1, j : j + 1]
        past = index >= start
        image = image + past.astype(I32)
        base = base + jnp.where(past, start - last, 0)
        last = start
    return image, index - base + CAP * image


def by_turn(base, up, down):
    return ((base, down, up), (up, base, down), (down, up, base))


def project_kernel(where, base, up, down, weight, far_weight, own, far):
    step = pl.program_id(0)
    depth = 3 * base.shape[2]
    for turn, held in enumerate(by_turn(base, up, down)):

        @pl.when(where[1] == turn)
        def _(held=held):
            left = jnp.concatenate([part[0] for part in held], axis=1)
            for block, out in ((weight, own), (far_weight, far)):
                term = mm(left, block[0, :, 0].reshape(depth, out.shape[1]))

                @pl.when(step == 0)
                def _(term=term, out=out):
                    out[...] = term

                @pl.when(step > 0)
                def _(term=term, out=out):
                    out[...] += term


def attend_kernel(own, far, cotangent, offsets, attention, grads):
    rows, slots = grads.shape[0], attention.shape[0]
    offs = offsets[...]
    image_col, slot_col = places(iota((rows, 1), 0), offs)
    image_row, slot_row = places(iota((1, rows), 1), offs)
    same = image_col == image_row
    cot = mm(hot(slot_col == iota((rows, slots), 1)), cotangent[...]).astype(BF16)
    rounded = (own[...] + far[...]).astype(BF16)
    query, key, value = rounded[:, :HD], rounded[:, HD : 2 * HD], rounded[:, 2 * HD :]
    scale = HD ** (-0.5)
    scores = mm(query, key, 1, 1) * scale
    expscore = jnp.where(same, jnp.exp(jnp.where(same, scores, 0.0)), 0.0)
    softmax = expscore / jnp.sum(expscore, axis=1, keepdims=True)
    weights = softmax.astype(BF16)
    result = mm(weights, value).astype(BF16)
    attention[...] = mm(hot(iota((slots, rows), 0) == slot_row), result).astype(BF16)
    d_value = mm(weights, cot, 0, 0)
    d_weights = mm(cot, value, 1, 1).astype(BF16).astype(F32)
    d_weights = jnp.where(same, d_weights, 0.0)
    inner = jnp.sum(d_weights * softmax, axis=1, keepdims=True)
    d_scores = (softmax * (d_weights - inner) * scale).astype(BF16)
    grads[:, :HD] = mm(d_scores, key).astype(BF16)
    grads[:, HD : 2 * HD] = mm(d_scores, query, 0, 0).astype(BF16)
    grads[:, 2 * HD :] = d_value.astype(BF16)


PICKS = (((0, 1), (4, 1), (5, 2), (3, 2)), ((2, 3), (0, 3), (1, 4), (5, 4)))


def split_kernel(where, base, up, down, out):
    row, col = iota((256, 128), 0), iota((256, 128), 1)
    low = hot(row == jnp.where(col < 64, col, col + 64))
    high = hot(row == jnp.where(col < 64, col + 64, col + 128))

    def spread(picks, held):
        def tile(group, t):
            return held[t // 2][group, :, (t % 2) * 128 : (t % 2) * 128 + 128]

        for x, (whole, cut) in enumerate(picks):
            for a in range(2):
                at = a * 384
                out[x, :, at : at + 128] = tile(2 * a, whole)
                out[x, :, at + 128 : at + 256] = tile(2 * a + 1, whole)
                both = jnp.concatenate([tile(2 * a, cut), tile(2 * a + 1, cut)], axis=1)
                out[x, :, at + 256 : at + 384] = mm(both, (low, high)[x % 2]).astype(BF16)

    for side, picks in enumerate(PICKS):
        for turn, held in enumerate(by_turn(base, up, down)):

            @pl.when((where[0] == side) & (where[1] == turn))
            def _(picks=picks, held=held):
                spread(picks, held)


def term_of(held, grads, a):
    depth = grads.shape[0] * grads.shape[1]
    left = held[:, :, a * 384 : a * 384 + 384].reshape(depth, 384)
    return mm(left, grads[...].reshape(depth, grads.shape[2]), 0, 0).astype(BF16)


def near_kernel(near, grads, out):
    for a in range(2):
        out[a] = term_of(near, grads, a)


def weight_kernel(where, near_terms, cross, grads, out):
    for source, side in ((0, where[0]), (1, 1 - where[0])):
        whole_side = jnp.where(where[4] == 1, 1 - side, side)
        for a in range(2):
            term = term_of(cross, grads, a) if source else near_terms[a]
            for b in range(2):
                group = 2 * a + b
                out[2 * group + whole_side, 0:128] = term[b * 128 : b * 128 + 128]
                out[2 * group + side, 128:192] = term[256 + b * 64 : 320 + b * 64]


def sum_kernel(odd, terms, out):
    total = terms[0].astype(F32)
    for k in range(1, terms.shape[0]):
        total += terms[k].astype(F32)

    @pl.when(odd[0] == 0)
    def _():
        out[...] = total

    @pl.when(odd[0] == 1)
    def _():
        out[0:64] = total[128:192]
        out[64:192] = total[0:128]


def params():
    return pltpu.CompilerParams(vmem_limit_bytes=40 * 1024 * 1024)


def cost(flops, moved):
    return pl.CostEstimate(flops=flops, bytes_accessed=moved, transcendentals=0)


VMEM = pl.BlockSpec(memory_space=pltpu.VMEM)
SMEM = pl.BlockSpec(memory_space=pltpu.SMEM)


def shards(patches, pack_route, pack_slot, project_weight, cotangent):
    owners, heads = lax.axis_size("dp"), lax.axis_size("mp")
    rows, width = patches.shape
    slots = cotangent.shape[0]
    cols = project_weight.shape[1]
    place = lax.axis_index("mp")
    turn = (place // 2) % 3
    x_index = lax.axis_index("dp") % X
    inner = (x_index == 1) | (x_index == 2)
    where = [place % 2, turn, (turn + 2) % 3, (turn + 1) % 3, inner]
    odd = (lax.axis_index("dp") % 2).astype(I32).reshape(1)
    where = jnp.stack([value.astype(I32) for value in where])
    along_x = [[y * X + x for x in range(X)] for y in range(Y)]
    along_y = [[y * X + x for y in range(Y)] for x in range(X)]

    outgoing = pl.pallas_call(
        send_kernel,
        out_shape=jax.ShapeDtypeStruct((owners * ROOM, width), BF16),
        in_specs=[pl.BlockSpec(memory_space=pl.ANY)] * 3,
        out_specs=VMEM,
        scratch_shapes=[
            pltpu.VMEM((rows, width), BF16),
            pltpu.VMEM((1, rows), I32),
            pltpu.VMEM((1, rows), I32),
            pltpu.SemaphoreType.DMA((3,)),
        ],
        compiler_params=pltpu.CompilerParams(vmem_limit_bytes=SEND_VMEM * 1024 * 1024),
        name="send",
    )(patches, pack_route.reshape(1, rows), pack_slot.reshape(1, rows))
    arrived = lax.all_to_all(outgoing.reshape(owners, ROOM, width), "dp", 0, 0, tiled=True)
    compact, offsets = pl.pallas_call(
        receive_kernel,
        out_shape=(
            jax.ShapeDtypeStruct((rows, width), BF16),
            jax.ShapeDtypeStruct((8, 128), I32),
        ),
        in_specs=[VMEM],
        out_specs=(VMEM, VMEM),
        compiler_params=params(),
        name="receive",
    )(arrived.reshape(owners * ROOM, width))

    thirds = [[6 * m + r for m in range(heads // 6)] for r in range(6)]

    def shift(block, by):
        return lax.ppermute(block, "mp", [(k, (k + by) % heads) for k in range(heads)])

    def swap(block):
        return lax.ppermute(block, "mp", [(k, k ^ 1) for k in range(heads)])

    far_weight = swap(project_weight)
    base = lax.all_gather(compact, "mp", axis=0, axis_index_groups=thirds)
    up, down = shift(base, 2), shift(base, -2)

    steps = heads // 6
    block = pl.BlockSpec((1, rows, width), lambda k, where: (k, 0, 0))
    weight_block = pl.BlockSpec((1, 3, 1, width, cols), lambda k, where: (k, 0, where[0], 0, 0))
    result = pl.BlockSpec((rows, cols), lambda k, where: (0, 0))
    own, far = pl.pallas_call(
        project_kernel,
        grid_spec=pltpu.PrefetchScalarGridSpec(
            num_scalar_prefetch=1,
            grid=(steps,),
            in_specs=[block] * 3 + [weight_block] * 2,
            out_specs=(result, result),
        ),
        out_shape=(jax.ShapeDtypeStruct((rows, cols), F32),) * 2,
        compiler_params=pltpu.CompilerParams(vmem_limit_bytes=PROJECT_VMEM * 1024 * 1024),
        cost_estimate=cost(2 * heads * rows * width * cols, 9 * 1024 * 1024),
        name="project",
    )(
        where, base, up, down,
        project_weight.reshape(steps, 3, 2, width, cols),
        far_weight.reshape(steps, 3, 2, width, cols),
    )
    own_far = swap(far)
    outbound = pl.pallas_call(
        split_kernel,
        out_shape=jax.ShapeDtypeStruct((X, rows, 768), BF16),
        in_specs=[SMEM] + [VMEM] * 3,
        out_specs=VMEM,
        compiler_params=params(),
        cost_estimate=cost(0, 4 * rows * 768 * 4),
        name="split",
    )(where, base, up, down)
    near = lax.all_to_all(outbound, "dp", 0, 0, axis_index_groups=along_x, tiled=True)
    attention, grads = pl.pallas_call(
        attend_kernel,
        out_shape=(
            jax.ShapeDtypeStruct((slots, HD), BF16),
            jax.ShapeDtypeStruct((rows, cols), BF16),
        ),
        in_specs=[VMEM] * 4,
        out_specs=(VMEM, VMEM),
        compiler_params=params(),
        cost_estimate=cost(2 * 9 * rows * rows * HD, 2 * 1024 * 1024),
        name="attend",
    )(own, own_far, cotangent, offsets)

    all_grads = lax.all_gather(grads, "dp", axis=0, axis_index_groups=along_x)
    near, all_grads = lax.optimization_barrier((near, all_grads))
    cross = swap(near)
    near_terms = pl.pallas_call(
        near_kernel,
        out_shape=jax.ShapeDtypeStruct((2, 384, cols), BF16),
        in_specs=[VMEM] * 2,
        out_specs=VMEM,
        compiler_params=params(),
        cost_estimate=cost(4 * rows * 1536 * cols, 3 * 1024 * 1024),
        name="near",
    )(near, all_grads)
    terms = pl.pallas_call(
        weight_kernel,
        out_shape=jax.ShapeDtypeStruct((Y, 192, cols), BF16),
        in_specs=[SMEM] + [VMEM] * 3,
        out_specs=VMEM,
        compiler_params=params(),
        cost_estimate=cost(2 * 4 * rows * 1536 * cols, 6 * 1024 * 1024),
        name="weight",
    )(where, near_terms, cross, all_grads)
    gathered = lax.all_to_all(terms, "dp", 0, 0, axis_index_groups=along_y, tiled=True)
    weight_grad = pl.pallas_call(
        sum_kernel,
        out_shape=jax.ShapeDtypeStruct((192, cols), F32),
        in_specs=[SMEM, VMEM],
        out_specs=VMEM,
        compiler_params=params(),
        name="sum",
    )(odd, gathered)
    return attention, weight_grad


def solution(mesh):
    in_specs = (P("dp", "mp"), P("dp", None), P("dp", None), P(None, "mp"), P("dp", "mp"))
    out_specs = (P("dp", "mp"), P("dp", "mp"))
    return jax.shard_map(shards, mesh=mesh, in_specs=in_specs, out_specs=out_specs, check_vma=False)
```

```python
import jax
import jax.numpy as jnp
from jax import lax
from jax.experimental import pallas as pl
from jax.experimental.pallas import tpu as pltpu
from jax.sharding import PartitionSpec as P

CAP = 96
HD = 128
SENT = 18
ROOM = 24
X, Y = 4, 8
PROJECT_VMEM = 48
SEND_VMEM = 60
F32, BF16, I32 = jnp.float32, jnp.bfloat16, jnp.int32


def iota(shape, dim):
    return lax.broadcasted_iota(I32, shape, dim)


def hot(condition):
    return jnp.where(condition, 1.0, 0.0).astype(BF16)


def mm(a, b, ca=1, cb=0):
    return lax.dot_general(a, b, (((ca,), (cb,)), ((), ())), preferred_element_type=F32)


def send_kernel(patches_in, route_in, slot_in, out, patches, route, slot, done):
    pairs = ((route_in, route), (slot_in, slot), (patches_in, patches))
    copies = [pltpu.make_async_copy(a, b, done.at[i]) for i, (a, b) in enumerate(pairs)]
    for copy in copies:
        copy.start()
    for copy in copies:
        copy.wait()
    rows = patches.shape[0]
    owners = out.shape[0] // ROOM
    pack = route[...]
    place = slot[...]
    matches = hot(pack == iota((owners, rows), 0))
    before = mm(matches, hot(iota((rows, rows), 0) < iota((rows, rows), 1)))
    matches = matches.astype(F32)
    position = jnp.sum(before * matches, axis=0, keepdims=True).astype(I32)
    total = mm(hot(pack * ROOM + position == iota((owners * ROOM, rows), 0)), patches[...])
    held = hot(position == iota((256, rows), 0))
    high = (matches * ((place >> 1) + 1).astype(F32)).astype(BF16)
    low = (matches * (place & 1).astype(F32)).astype(BF16)
    line, owner = iota((owners * ROOM, owners), 0), iota((owners * ROOM, owners), 1)
    for row, part in ((SENT, high), (SENT + 1, low)):
        total += mm(hot(line == owner * ROOM + row), mm(part, held, 1, 1).astype(BF16))
    out[...] = total.astype(BF16)


def receive_kernel(arrived, out, offsets):
    lines = arrived.shape[0]
    owners = lines // ROOM
    rows = out.shape[0]
    data = arrived[...]
    line, owner = iota((owners, lines), 1), iota((owners, lines), 0)
    spread = hot((line >= owner * ROOM) & (line < owner * ROOM + ROOM))
    within = jnp.sum(
        jnp.where((line >= owner * ROOM) & (line < owner * ROOM + ROOM), line - owner * ROOM, 0),
        axis=0,
        keepdims=True,
    )
    chosen = iota((128, lines), 0) == within
    number = []
    for row in (SENT, SENT + 1):
        part = mm(hot(line == owner * ROOM + row), data)[:, :128].astype(BF16)
        wide = mm(part, spread, 0, 0)
        number.append(jnp.sum(jnp.where(chosen, wide, 0.0), axis=0, keepdims=True).astype(I32))
    live = (number[0] > 0) & (within < SENT)
    place = 2 * (number[0] - 1) + number[1]
    image = sum((place >= CAP * j).astype(I32) for j in (1, 2, 3))
    start, starts, base = jnp.zeros((1, 1), I32), [], jnp.zeros_like(place)
    for j in range(3):
        count = jnp.sum(jnp.where(live & (image == j), 1.0, 0.0), axis=1, keepdims=True)
        start = start + count.astype(I32)
        starts.append(start)
        base = jnp.where(image == j + 1, start, base)
    target = jnp.where(live, base + place - CAP * image, -1)
    out[...] = mm(hot(iota((rows, lines), 0) == target), data).astype(BF16)
    lane = iota((8, 128), 1)
    offsets[...] = sum(jnp.where(lane == j, starts[j], 0) for j in range(3))


def places(index, offsets):
    image, base, last = 0, 0, 0
    for j in range(3):
        start = offsets[0:1, j : j + 1]
        past = index >= start
        image = image + past.astype(I32)
        base = base + jnp.where(past, start - last, 0)
        last = start
    return image, index - base + CAP * image


def by_turn(base, up, down):
    return ((base, down, up), (up, base, down), (down, up, base))


def project_kernel(where, base, up, down, weight, far_weight, own, far):
    step = pl.program_id(0)
    depth = 3 * base.shape[2]
    for turn, held in enumerate(by_turn(base, up, down)):

        @pl.when(where[1] == turn)
        def _(held=held):
            left = jnp.concatenate([part[0] for part in held], axis=1)
            for block, out in ((weight, own), (far_weight, far)):
                term = mm(left, block[0, :, 0].reshape(depth, out.shape[1]))

                @pl.when(step == 0)
                def _(term=term, out=out):
                    out[...] = term

                @pl.when(step > 0)
                def _(term=term, out=out):
                    out[...] += term


def attend_kernel(own, far, cotangent, offsets, attention, grads):
    rows, slots = grads.shape[0], attention.shape[0]
    offs = offsets[...]
    image_col, slot_col = places(iota((rows, 1), 0), offs)
    image_row, slot_row = places(iota((1, rows), 1), offs)
    same = image_col == image_row
    cot = mm(hot(slot_col == iota((rows, slots), 1)), cotangent[...]).astype(BF16)
    rounded = (own[...] + far[...]).astype(BF16)
    query, key, value = rounded[:, :HD], rounded[:, HD : 2 * HD], rounded[:, 2 * HD :]
    scale = HD ** (-0.5)
    scores = mm(query, key, 1, 1) * scale
    expscore = jnp.where(same, jnp.exp(jnp.where(same, scores, 0.0)), 0.0)
    softmax = expscore / jnp.sum(expscore, axis=1, keepdims=True)
    weights = softmax.astype(BF16)
    result = mm(weights, value).astype(BF16)
    attention[...] = mm(hot(iota((slots, rows), 0) == slot_row), result).astype(BF16)
    d_value = mm(weights, cot, 0, 0)
    d_weights = mm(cot, value, 1, 1).astype(BF16).astype(F32)
    d_weights = jnp.where(same, d_weights, 0.0)
    inner = jnp.sum(d_weights * softmax, axis=1, keepdims=True)
    d_scores = (softmax * (d_weights - inner) * scale).astype(BF16)
    grads[:, :HD] = mm(d_scores, key).astype(BF16)
    grads[:, HD : 2 * HD] = mm(d_scores, query, 0, 0).astype(BF16)
    grads[:, 2 * HD :] = d_value.astype(BF16)


PICKS = (((0, 1), (4, 1), (5, 2), (3, 2)), ((2, 3), (0, 3), (1, 4), (5, 4)))


def split_kernel(where, base, up, down, out):
    row, col = iota((256, 128), 0), iota((256, 128), 1)
    low = hot(row == jnp.where(col < 64, col, col + 64))
    high = hot(row == jnp.where(col < 64, col + 64, col + 128))

    def spread(picks, held):
        def tile(group, t):
            return held[t // 2][group, :, (t % 2) * 128 : (t % 2) * 128 + 128]

        for x, (whole, cut) in enumerate(picks):
            out[x, :, 0:128] = tile(0, whole)
            out[x, :, 128:256] = tile(1, whole)
            both = jnp.concatenate([tile(0, cut), tile(1, cut)], axis=1)
            out[x, :, 256:384] = mm(both, (low, high)[x % 2]).astype(BF16)

    for side, picks in enumerate(PICKS):
        for turn, held in enumerate(by_turn(base, up, down)):

            @pl.when((where[0] == side) & (where[1] == turn))
            def _(picks=picks, held=held):
                spread(picks, held)


def term_of(held, grads, a):
    depth = grads.shape[0] * grads.shape[1]
    left = held[:, :, a * 384 : a * 384 + 384].reshape(depth, 384)
    return mm(left, grads[...].reshape(depth, grads.shape[2]), 0, 0).astype(BF16)


def near_kernel(near, grads, out):
    for a in range(2):
        out[a] = term_of(near, grads, a)


def weight_kernel(where, near_terms, cross, grads, out):
    for term, side in ((near_terms[0], where[0]), (term_of(cross, grads, 0), 1 - where[0])):
        whole_side = jnp.where(where[4] == 1, 1 - side, side)
        for b in range(2):
            out[2 * b + whole_side, 0:128] = term[b * 128 : b * 128 + 128]
            out[2 * b + side, 128:192] = term[256 + b * 64 : 320 + b * 64]


def sum_kernel(odd, terms, out):
    total = terms[0].astype(F32)
    for k in range(1, terms.shape[0]):
        total += terms[k].astype(F32)

    @pl.when(odd[0] == 0)
    def _():
        out[...] = total

    @pl.when(odd[0] == 1)
    def _():
        out[0:64] = total[128:192]
        out[64:192] = total[0:128]


def params():
    return pltpu.CompilerParams(vmem_limit_bytes=40 * 1024 * 1024)


def cost(flops, moved):
    return pl.CostEstimate(flops=flops, bytes_accessed=moved, transcendentals=0)


VMEM = pl.BlockSpec(memory_space=pltpu.VMEM)
SMEM = pl.BlockSpec(memory_space=pltpu.SMEM)


def shards(patches, pack_route, pack_slot, project_weight, cotangent):
    owners, heads = lax.axis_size("dp"), lax.axis_size("mp")
    rows, width = patches.shape
    slots = cotangent.shape[0]
    cols = project_weight.shape[1]
    place = lax.axis_index("mp")
    turn = (place // 2) % 3
    x_index = lax.axis_index("dp") % X
    inner = (x_index == 1) | (x_index == 2)
    where = [place % 2, turn, (turn + 2) % 3, (turn + 1) % 3, inner]
    odd = (lax.axis_index("dp") % 2).astype(I32).reshape(1)
    where = jnp.stack([value.astype(I32) for value in where])
    along_x = [[y * X + x for x in range(X)] for y in range(Y)]
    along_y = [[y * X + x for y in range(Y)] for x in range(X)]

    outgoing = pl.pallas_call(
        send_kernel,
        out_shape=jax.ShapeDtypeStruct((owners * ROOM, width), BF16),
        in_specs=[pl.BlockSpec(memory_space=pl.ANY)] * 3,
        out_specs=VMEM,
        scratch_shapes=[
            pltpu.VMEM((rows, width), BF16),
            pltpu.VMEM((1, rows), I32),
            pltpu.VMEM((1, rows), I32),
            pltpu.SemaphoreType.DMA((3,)),
        ],
        compiler_params=pltpu.CompilerParams(vmem_limit_bytes=SEND_VMEM * 1024 * 1024),
        name="send",
    )(patches, pack_route.reshape(1, rows), pack_slot.reshape(1, rows))
    arrived = lax.all_to_all(outgoing.reshape(owners, ROOM, width), "dp", 0, 0, tiled=True)
    compact, offsets = pl.pallas_call(
        receive_kernel,
        out_shape=(
            jax.ShapeDtypeStruct((rows, width), BF16),
            jax.ShapeDtypeStruct((8, 128), I32),
        ),
        in_specs=[VMEM],
        out_specs=(VMEM, VMEM),
        compiler_params=params(),
        name="receive",
    )(arrived.reshape(owners * ROOM, width))

    thirds = [[6 * m + r for m in range(heads // 6)] for r in range(6)]

    def shift(block, by):
        return lax.ppermute(block, "mp", [(k, (k + by) % heads) for k in range(heads)])

    def swap(block):
        return lax.ppermute(block, "mp", [(k, k ^ 1) for k in range(heads)])

    far_weight = swap(project_weight)
    base = lax.all_gather(compact, "mp", axis=0, axis_index_groups=thirds)
    up, down = shift(base, 2), shift(base, -2)

    steps = heads // 6
    block = pl.BlockSpec((1, rows, width), lambda k, where: (k, 0, 0))
    weight_block = pl.BlockSpec((1, 3, 1, width, cols), lambda k, where: (k, 0, where[0], 0, 0))
    result = pl.BlockSpec((rows, cols), lambda k, where: (0, 0))
    own, far = pl.pallas_call(
        project_kernel,
        grid_spec=pltpu.PrefetchScalarGridSpec(
            num_scalar_prefetch=1,
            grid=(steps,),
            in_specs=[block] * 3 + [weight_block] * 2,
            out_specs=(result, result),
        ),
        out_shape=(jax.ShapeDtypeStruct((rows, cols), F32),) * 2,
        compiler_params=pltpu.CompilerParams(vmem_limit_bytes=PROJECT_VMEM * 1024 * 1024),
        cost_estimate=cost(2 * heads * rows * width * cols, 9 * 1024 * 1024),
        name="project",
    )(
        where, base, up, down,
        project_weight.reshape(steps, 3, 2, width, cols),
        far_weight.reshape(steps, 3, 2, width, cols),
    )
    own_far = swap(far)
    pair = pl.BlockSpec((2, rows, width), lambda a, where: (a, 0, 0))
    outbound = pl.pallas_call(
        split_kernel,
        grid_spec=pltpu.PrefetchScalarGridSpec(
            num_scalar_prefetch=1,
            grid=(2,),
            in_specs=[pair] * 3,
            out_specs=pl.BlockSpec((X, rows, 384), lambda a, where: (0, 0, a)),
        ),
        out_shape=jax.ShapeDtypeStruct((X, rows, 768), BF16),
        compiler_params=params(),
        cost_estimate=cost(0, 4 * rows * 768 * 4),
        name="split",
    )(where, base, up, down)
    near = lax.all_to_all(outbound, "dp", 0, 0, axis_index_groups=along_x, tiled=True)
    attention, grads = pl.pallas_call(
        attend_kernel,
        out_shape=(
            jax.ShapeDtypeStruct((slots, HD), BF16),
            jax.ShapeDtypeStruct((rows, cols), BF16),
        ),
        in_specs=[VMEM] * 4,
        out_specs=(VMEM, VMEM),
        compiler_params=params(),
        cost_estimate=cost(2 * 9 * rows * rows * HD, 2 * 1024 * 1024),
        name="attend",
    )(own, own_far, cotangent, offsets)

    all_grads = lax.all_gather(grads, "dp", axis=0, axis_index_groups=along_x)
    near, all_grads = lax.optimization_barrier((near, all_grads))
    cross = swap(near)
    near_terms = pl.pallas_call(
        near_kernel,
        out_shape=jax.ShapeDtypeStruct((2, 384, cols), BF16),
        in_specs=[VMEM] * 2,
        out_specs=VMEM,
        compiler_params=params(),
        cost_estimate=cost(4 * rows * 1536 * cols, 3 * 1024 * 1024),
        name="near",
    )(near, all_grads)
    terms = pl.pallas_call(
        weight_kernel,
        grid_spec=pltpu.PrefetchScalarGridSpec(
            num_scalar_prefetch=1,
            grid=(2,),
            in_specs=[
                pl.BlockSpec((1, 384, cols), lambda a, where: (a, 0, 0)),
                pl.BlockSpec((X, rows, 384), lambda a, where: (0, 0, a)),
                pl.BlockSpec((X, rows, cols), lambda a, where: (0, 0, 0)),
            ],
            out_specs=pl.BlockSpec((4, 192, cols), lambda a, where: (a, 0, 0)),
        ),
        out_shape=jax.ShapeDtypeStruct((Y, 192, cols), BF16),
        compiler_params=params(),
        cost_estimate=cost(4 * rows * 1536 * cols, 6 * 1024 * 1024),
        name="weight",
    )(where, near_terms, cross, all_grads)
    gathered = lax.all_to_all(terms, "dp", 0, 0, axis_index_groups=along_y, tiled=True)
    weight_grad = pl.pallas_call(
        sum_kernel,
        out_shape=jax.ShapeDtypeStruct((192, cols), F32),
        in_specs=[SMEM, VMEM],
        out_specs=VMEM,
        compiler_params=params(),
        name="sum",
    )(odd, gathered)
    return attention, weight_grad


def solution(mesh):
    in_specs = (P("dp", "mp"), P("dp", None), P("dp", None), P(None, "mp"), P("dp", "mp"))
    out_specs = (P("dp", "mp"), P("dp", "mp"))
    return jax.shard_map(shards, mesh=mesh, in_specs=in_specs, out_specs=out_specs, check_vma=False)
```

```python
import jax
import jax.numpy as jnp
from jax import lax
from jax.experimental import pallas as pl
from jax.experimental.pallas import tpu as pltpu
from jax.sharding import PartitionSpec as P

CAP = 96
HD = 128
SENT = 18
ROOM = 24
X, Y = 4, 8
PROJECT_VMEM = 48
SEND_VMEM = 60
F32, BF16, I32 = jnp.float32, jnp.bfloat16, jnp.int32


def iota(shape, dim):
    return lax.broadcasted_iota(I32, shape, dim)


def hot(condition):
    return jnp.where(condition, 1.0, 0.0).astype(BF16)


def mm(a, b, ca=1, cb=0):
    return lax.dot_general(a, b, (((ca,), (cb,)), ((), ())), preferred_element_type=F32)


def send_kernel(patches_in, route_in, slot_in, out, patches, route, slot, done):
    pairs = ((route_in, route), (slot_in, slot), (patches_in, patches))
    copies = [pltpu.make_async_copy(a, b, done.at[i]) for i, (a, b) in enumerate(pairs)]
    for copy in copies:
        copy.start()
    for copy in copies:
        copy.wait()
    rows = patches.shape[0]
    owners = out.shape[0] // ROOM
    pack = route[...]
    place = slot[...]
    matches = hot(pack == iota((owners, rows), 0))
    before = mm(matches, hot(iota((rows, rows), 0) < iota((rows, rows), 1)))
    matches = matches.astype(F32)
    position = jnp.sum(before * matches, axis=0, keepdims=True).astype(I32)
    total = mm(hot(pack * ROOM + position == iota((owners * ROOM, rows), 0)), patches[...])
    held = hot(position == iota((256, rows), 0))
    high = (matches * ((place >> 1) + 1).astype(F32)).astype(BF16)
    low = (matches * (place & 1).astype(F32)).astype(BF16)
    line, owner = iota((owners * ROOM, owners), 0), iota((owners * ROOM, owners), 1)
    for row, part in ((SENT, high), (SENT + 1, low)):
        total += mm(hot(line == owner * ROOM + row), mm(part, held, 1, 1).astype(BF16))
    out[...] = total.astype(BF16)


def receive_kernel(arrived, out, offsets):
    lines = arrived.shape[0]
    owners = lines // ROOM
    rows = out.shape[0]
    data = arrived[...]
    line, owner = iota((owners, lines), 1), iota((owners, lines), 0)
    spread = hot((line >= owner * ROOM) & (line < owner * ROOM + ROOM))
    within = jnp.sum(
        jnp.where((line >= owner * ROOM) & (line < owner * ROOM + ROOM), line - owner * ROOM, 0),
        axis=0,
        keepdims=True,
    )
    chosen = iota((128, lines), 0) == within
    number = []
    for row in (SENT, SENT + 1):
        part = mm(hot(line == owner * ROOM + row), data)[:, :128].astype(BF16)
        wide = mm(part, spread, 0, 0)
        number.append(jnp.sum(jnp.where(chosen, wide, 0.0), axis=0, keepdims=True).astype(I32))
    live = (number[0] > 0) & (within < SENT)
    place = 2 * (number[0] - 1) + number[1]
    image = sum((place >= CAP * j).astype(I32) for j in (1, 2, 3))
    start, starts, base = jnp.zeros((1, 1), I32), [], jnp.zeros_like(place)
    for j in range(3):
        count = jnp.sum(jnp.where(live & (image == j), 1.0, 0.0), axis=1, keepdims=True)
        start = start + count.astype(I32)
        starts.append(start)
        base = jnp.where(image == j + 1, start, base)
    target = jnp.where(live, base + place - CAP * image, -1)
    out[...] = mm(hot(iota((rows, lines), 0) == target), data).astype(BF16)
    lane = iota((8, 128), 1)
    offsets[...] = sum(jnp.where(lane == j, starts[j], 0) for j in range(3))


def places(index, offsets):
    image, base, last = 0, 0, 0
    for j in range(3):
        start = offsets[0:1, j : j + 1]
        past = index >= start
        image = image + past.astype(I32)
        base = base + jnp.where(past, start - last, 0)
        last = start
    return image, index - base + CAP * image


def by_turn(base, up, down):
    return ((base, down, up), (up, base, down), (down, up, base))


def project_kernel(where, base, up, down, *refs):
    own, far = refs[6:]
    step = pl.program_id(0)
    for turn, held in enumerate(by_turn(base, up, down)):

        @pl.when(where[1] == turn)
        def _(held=held):
            for blocks, out in ((refs[:3], own), (refs[3:6], far)):
                term = sum(mm(part[0], block[0, 0, 0]) for part, block in zip(held, blocks))

                @pl.when(step == 0)
                def _(term=term, out=out):
                    out[...] = term

                @pl.when(step > 0)
                def _(term=term, out=out):
                    out[...] += term


def attend_kernel(own, far, cotangent, offsets, attention, grads):
    rows, slots = grads.shape[0], attention.shape[0]
    offs = offsets[...]
    image_col, slot_col = places(iota((rows, 1), 0), offs)
    image_row, slot_row = places(iota((1, rows), 1), offs)
    same = image_col == image_row
    cot = mm(hot(slot_col == iota((rows, slots), 1)), cotangent[...]).astype(BF16)
    rounded = (own[...] + far[...]).astype(BF16)
    query, key, value = rounded[:, :HD], rounded[:, HD : 2 * HD], rounded[:, 2 * HD :]
    scale = HD ** (-0.5)
    scores = mm(query, key, 1, 1) * scale
    expscore = jnp.where(same, jnp.exp(jnp.where(same, scores, 0.0)), 0.0)
    softmax = expscore / jnp.sum(expscore, axis=1, keepdims=True)
    weights = softmax.astype(BF16)
    result = mm(weights, value).astype(BF16)
    attention[...] = mm(hot(iota((slots, rows), 0) == slot_row), result).astype(BF16)
    d_value = mm(weights, cot, 0, 0)
    d_weights = mm(cot, value, 1, 1).astype(BF16).astype(F32)
    d_weights = jnp.where(same, d_weights, 0.0)
    inner = jnp.sum(d_weights * softmax, axis=1, keepdims=True)
    d_scores = (softmax * (d_weights - inner) * scale).astype(BF16)
    grads[:, :HD] = mm(d_scores, key).astype(BF16)
    grads[:, HD : 2 * HD] = mm(d_scores, query, 0, 0).astype(BF16)
    grads[:, 2 * HD :] = d_value.astype(BF16)


PICKS = (((0, 1), (4, 1), (5, 2), (3, 2)), ((2, 3), (0, 3), (1, 4), (5, 4)))


def split_kernel(where, base, up, down, out):
    row, col = iota((256, 128), 0), iota((256, 128), 1)
    low = hot(row == jnp.where(col < 64, col, col + 64))
    high = hot(row == jnp.where(col < 64, col + 64, col + 128))

    def spread(picks, held):
        def tile(group, t):
            return held[t // 2][group, :, (t % 2) * 128 : (t % 2) * 128 + 128]

        for x, (whole, cut) in enumerate(picks):
            for a in range(2):
                at = a * 384
                out[x, :, at : at + 128] = tile(2 * a, whole)
                out[x, :, at + 128 : at + 256] = tile(2 * a + 1, whole)
                both = jnp.concatenate([tile(2 * a, cut), tile(2 * a + 1, cut)], axis=1)
                out[x, :, at + 256 : at + 384] = mm(both, (low, high)[x % 2]).astype(BF16)

    for side, picks in enumerate(PICKS):
        for turn, held in enumerate(by_turn(base, up, down)):

            @pl.when((where[0] == side) & (where[1] == turn))
            def _(picks=picks, held=held):
                spread(picks, held)


def term_of(held, grads, a):
    depth = grads.shape[0] * grads.shape[1]
    left = held[:, :, a * 384 : a * 384 + 384].reshape(depth, 384)
    return mm(left, grads[...].reshape(depth, grads.shape[2]), 0, 0).astype(BF16)


def near_kernel(near, grads, out):
    for a in range(2):
        out[a] = term_of(near, grads, a)


def weight_kernel(where, near_terms, cross, grads, out):
    for source, side in ((0, where[0]), (1, 1 - where[0])):
        whole_side = jnp.where(where[4] == 1, 1 - side, side)
        for a in range(2):
            term = term_of(cross, grads, a) if source else near_terms[a]
            for b in range(2):
                group = 2 * a + b
                out[2 * group + whole_side, 0:128] = term[b * 128 : b * 128 + 128]
                out[2 * group + side, 128:192] = term[256 + b * 64 : 320 + b * 64]


def sum_kernel(odd, terms, out):
    total = terms[0].astype(F32)
    for k in range(1, terms.shape[0]):
        total += terms[k].astype(F32)

    @pl.when(odd[0] == 0)
    def _():
        out[...] = total

    @pl.when(odd[0] == 1)
    def _():
        out[0:64] = total[128:192]
        out[64:192] = total[0:128]


def params():
    return pltpu.CompilerParams(vmem_limit_bytes=40 * 1024 * 1024)


def cost(flops, moved):
    return pl.CostEstimate(flops=flops, bytes_accessed=moved, transcendentals=0)


VMEM = pl.BlockSpec(memory_space=pltpu.VMEM)
SMEM = pl.BlockSpec(memory_space=pltpu.SMEM)


def shards(patches, pack_route, pack_slot, project_weight, cotangent):
    owners, heads = lax.axis_size("dp"), lax.axis_size("mp")
    rows, width = patches.shape
    slots = cotangent.shape[0]
    cols = project_weight.shape[1]
    place = lax.axis_index("mp")
    turn = (place // 2) % 3
    x_index = lax.axis_index("dp") % X
    inner = (x_index == 1) | (x_index == 2)
    where = [place % 2, turn, (turn + 2) % 3, (turn + 1) % 3, inner]
    odd = (lax.axis_index("dp") % 2).astype(I32).reshape(1)
    where = jnp.stack([value.astype(I32) for value in where])
    along_x = [[y * X + x for x in range(X)] for y in range(Y)]
    along_y = [[y * X + x for y in range(Y)] for x in range(X)]

    outgoing = pl.pallas_call(
        send_kernel,
        out_shape=jax.ShapeDtypeStruct((owners * ROOM, width), BF16),
        in_specs=[pl.BlockSpec(memory_space=pl.ANY)] * 3,
        out_specs=VMEM,
        scratch_shapes=[
            pltpu.VMEM((rows, width), BF16),
            pltpu.VMEM((1, rows), I32),
            pltpu.VMEM((1, rows), I32),
            pltpu.SemaphoreType.DMA((3,)),
        ],
        compiler_params=pltpu.CompilerParams(vmem_limit_bytes=SEND_VMEM * 1024 * 1024),
        name="send",
    )(patches, pack_route.reshape(1, rows), pack_slot.reshape(1, rows))
    arrived = lax.all_to_all(outgoing.reshape(owners, ROOM, width), "dp", 0, 0, tiled=True)
    compact, offsets = pl.pallas_call(
        receive_kernel,
        out_shape=(
            jax.ShapeDtypeStruct((rows, width), BF16),
            jax.ShapeDtypeStruct((8, 128), I32),
        ),
        in_specs=[VMEM],
        out_specs=(VMEM, VMEM),
        compiler_params=params(),
        name="receive",
    )(arrived.reshape(owners * ROOM, width))

    thirds = [[6 * m + r for m in range(heads // 6)] for r in range(6)]

    def shift(block, by):
        return lax.ppermute(block, "mp", [(k, (k + by) % heads) for k in range(heads)])

    def swap(block):
        return lax.ppermute(block, "mp", [(k, k ^ 1) for k in range(heads)])

    far_weight = swap(project_weight)
    base = lax.all_gather(compact, "mp", axis=0, axis_index_groups=thirds)
    up, down = shift(base, 2), shift(base, -2)

    steps = heads // 6
    block = pl.BlockSpec((1, rows, width), lambda k, where: (k, 0, 0))
    weight_blocks = [
        pl.BlockSpec((1, 1, 1, width, cols), lambda k, where, t=t: (k, t, where[0], 0, 0))
        for t in range(3)
    ]
    result = pl.BlockSpec((rows, cols), lambda k, where: (0, 0))
    own, far = pl.pallas_call(
        project_kernel,
        grid_spec=pltpu.PrefetchScalarGridSpec(
            num_scalar_prefetch=1,
            grid=(steps,),
            in_specs=[block] * 3 + weight_blocks * 2,
            out_specs=(result, result),
        ),
        out_shape=(jax.ShapeDtypeStruct((rows, cols), F32),) * 2,
        compiler_params=pltpu.CompilerParams(vmem_limit_bytes=PROJECT_VMEM * 1024 * 1024),
        cost_estimate=cost(2 * heads * rows * width * cols, 9 * 1024 * 1024),
        name="project",
    )(
        where, base, up, down,
        *[project_weight.reshape(steps, 3, 2, width, cols)] * 3,
        *[far_weight.reshape(steps, 3, 2, width, cols)] * 3,
    )
    own_far = swap(far)
    outbound = pl.pallas_call(
        split_kernel,
        out_shape=jax.ShapeDtypeStruct((X, rows, 768), BF16),
        in_specs=[SMEM] + [VMEM] * 3,
        out_specs=VMEM,
        compiler_params=params(),
        cost_estimate=cost(0, 4 * rows * 768 * 4),
        name="split",
    )(where, base, up, down)
    near = lax.all_to_all(outbound, "dp", 0, 0, axis_index_groups=along_x, tiled=True)
    attention, grads = pl.pallas_call(
        attend_kernel,
        out_shape=(
            jax.ShapeDtypeStruct((slots, HD), BF16),
            jax.ShapeDtypeStruct((rows, cols), BF16),
        ),
        in_specs=[VMEM] * 4,
        out_specs=(VMEM, VMEM),
        compiler_params=params(),
        cost_estimate=cost(2 * 9 * rows * rows * HD, 2 * 1024 * 1024),
        name="attend",
    )(own, own_far, cotangent, offsets)

    all_grads = lax.all_gather(grads, "dp", axis=0, axis_index_groups=along_x)
    near, all_grads = lax.optimization_barrier((near, all_grads))
    cross = swap(near)
    near_terms = pl.pallas_call(
        near_kernel,
        out_shape=jax.ShapeDtypeStruct((2, 384, cols), BF16),
        in_specs=[VMEM] * 2,
        out_specs=VMEM,
        compiler_params=params(),
        cost_estimate=cost(4 * rows * 1536 * cols, 3 * 1024 * 1024),
        name="near",
    )(near, all_grads)
    terms = pl.pallas_call(
        weight_kernel,
        out_shape=jax.ShapeDtypeStruct((Y, 192, cols), BF16),
        in_specs=[SMEM] + [VMEM] * 3,
        out_specs=VMEM,
        compiler_params=params(),
        cost_estimate=cost(2 * 4 * rows * 1536 * cols, 6 * 1024 * 1024),
        name="weight",
    )(where, near_terms, cross, all_grads)
    gathered = lax.all_to_all(terms, "dp", 0, 0, axis_index_groups=along_y, tiled=True)
    weight_grad = pl.pallas_call(
        sum_kernel,
        out_shape=jax.ShapeDtypeStruct((192, cols), F32),
        in_specs=[SMEM, VMEM],
        out_specs=VMEM,
        compiler_params=params(),
        name="sum",
    )(odd, gathered)
    return attention, weight_grad


def solution(mesh):
    in_specs = (P("dp", "mp"), P("dp", None), P("dp", None), P(None, "mp"), P("dp", "mp"))
    out_specs = (P("dp", "mp"), P("dp", "mp"))
    return jax.shard_map(shards, mesh=mesh, in_specs=in_specs, out_specs=out_specs, check_vma=False)
```
